128 devices in a mesh: chan: 32 (over y, z, core), tm: 4 (over x).
Axes of the slice: x: 4, y: 4, z: 4, core: 2. Of those that a mesh axis runs over, the one named last changes fastest.
Arguments:
- records: bfloat16 [16, 1920, 4096], P('tm', 'chan'), may hold values from -6 to 6
- quality: int32 [16, 4096], P('tm', 'chan'), may hold values 0 or 1
- tile_list: int32 [96, 2], replicated, may hold values from 0 to 31, as said below
- tile_slot_owner: int32 [96], replicated, may hold values from 0 to 191, as said below
Outputs:
- correlations: float32 [192, 16, 128, 512], P('chan', 'tm')
The draws below stay inside these ranges and needn't reach their ends.
Inputs may be any that keep to these rules, and one draw needn't show every extreme that they name: `tile_list`: row t holds source block t // 3 and a receiver block within 2 blocks of it along the looped fibre (mod 32); the receivers of one source block are distinct. `tile_slot_owner`: entry t is owner * 6 + slot; the tiles of source block b are owned by block b's device or device b + 1 (mod 32); no slot holds two tiles; some device owns exactly 6 tiles.
All inputs are finite; a program needn't handle non-finite values. No bound on the sum of `quality` on one device may be relied on, other than what follows from the above.
Results may differ from the reference program's by a relative error of at most 0.015.
Values may be sent and summed in bfloat16 or wider, within the bound.
No kernel may reach another device: no remote copies, remote signals or barrier semaphores. Data moves between devices by JAX's collectives and lax.ppermute only.
A program may use at most 192 MiB of HBM per device.

```python
import math
import jax
import jax.numpy as jnp
from jax import lax

L = 1920
F = 768
K0 = 8
HALF = 32
LAG_COUNT = 512
BLOCK_CHANNELS = 128
VIRTUAL_SOURCES = 16
TPS = 3
REACH = 2
SEG_DEV = 4
SEGS = 16
NB = 32
CH = 4096
TCAP = 6
SLOT_TOTAL = 192


def draw_tile_list(key, part):
    key = jax.random.fold_in(key, 11)
    span = 2 * REACH + 1
    scores = jax.random.randint(key, (NB, span), 0, 1 << 20) * span + jnp.arange(span, dtype=jnp.int32)[None, :]
    rank_order = jnp.argsort(scores, axis=1, stable=True)[:, :TPS]
    offsets = jnp.sort(rank_order, axis=1).astype(jnp.int32) - REACH
    sources = jnp.broadcast_to(jnp.arange(NB, dtype=jnp.int32)[:, None], (NB, TPS))
    receivers = jnp.mod(sources + offsets, NB)
    return jnp.stack([sources.reshape(-1), receivers.reshape(-1)], axis=1).astype(jnp.int32)


def draw_tile_slot_owner(key, part):
    key = jax.random.fold_in(key, 23)
    key_moved, key_full = jax.random.split(key)
    moved_count = jax.random.randint(key_moved, (NB,), 0, TPS + 1)
    full_device = jax.random.randint(key_full, (), 0, NB)
    moved_count = moved_count.at[full_device].set(0)
    moved_count = moved_count.at[jnp.mod(full_device - 1, NB)].set(TPS)
    stay_count = TPS - moved_count
    sources = jnp.arange(NB, dtype=jnp.int32)[:, None]
    column = jnp.arange(TPS, dtype=jnp.int32)[None, :]
    next_block = jnp.mod(sources + 1, NB)
    stay_next = jnp.roll(stay_count, -1)[:, None]
    stays_home = column < stay_count[:, None]
    owner_device = jnp.where(stays_home, sources, next_block)
    slot_index = jnp.where(stays_home, column, stay_next + column - stay_count[:, None])
    return (owner_device * TCAP + slot_index).reshape(-1).astype(jnp.int32)


def touch_ends(values, rng, smallest, high):
    longest = values.shape.index(max(values.shape))
    spots = []
    for shift in (0, 1):
        where = [jax.random.randint(jax.random.fold_in(rng, axis), (), 0, length) for axis, length in enumerate(values.shape)]
        where[longest] = (where[longest] + shift) % values.shape[longest]
        spots.append(tuple(where))
    return values.at[spots[0]].set(smallest).at[spots[1]].set(high)


def block_scale(stream_key, dims, pieces, low, high):
    factor_of, own = 1.0, jax.random.fold_in(stream_key, 6)
    for dim, shards_of in pieces:
        heights = jnp.exp(jax.random.uniform(jax.random.fold_in(own, dim), (shards_of,), jnp.float32, low / len(pieces), high / len(pieces)))
        factor_of = factor_of * jnp.repeat(heights, dims[dim] // shards_of).reshape([-1 if axis == dim else 1 for axis in range(len(dims))])
    return factor_of


def normal_values(own_key, dims, width, limit, cuts=(), kind=jnp.bfloat16):
    loudness = block_scale(own_key, dims, cuts, -0.22, 0.18) if cuts else 1.0
    drawn = jax.random.normal(own_key, dims, jnp.float32) * width * loudness
    return jnp.minimum(jnp.maximum(drawn, -limit), limit).astype(kind)


def setup_inputs(seed: int = 0) -> dict:
    key_of = jax.random.split(jax.random.key(seed), 5)
    records = normal_values(key_of[0], (SEGS, L, CH), 1.0, 6.0, ((0, 4), (1, 32)))
    quality = touch_ends((jax.random.randint(key_of[1], (SEGS, CH), 0, 8) < 7).astype(jnp.int32), jax.random.fold_in(key_of[1], 1), 0, 1)
    tile_list = draw_tile_list(jax.random.fold_in(key_of[4], 71), 0)
    tile_slot_owner = draw_tile_slot_owner(jax.random.fold_in(key_of[4], 71), 0)
    return {"records": records, "quality": quality, "tile_list": tile_list, "tile_slot_owner": tile_slot_owner}


def forward_table():
    samples = jnp.arange(L, dtype=jnp.int32)[:, None]
    bins = K0 + jnp.arange(F, dtype=jnp.int32)[None, :]
    angles = jnp.mod(samples * bins, L).astype(jnp.float32) * (2.0 * math.pi / L)
    window = 0.5 - 0.5 * jnp.cos(jnp.arange(L, dtype=jnp.int32).astype(jnp.float32) * (2.0 * math.pi / L))
    return jnp.concatenate([jnp.cos(angles), -jnp.sin(angles)], axis=1) * window[:, None]

def smoothing():
    indices = jnp.arange(F, dtype=jnp.int32)
    in_window = (jnp.abs(indices[:, None] - indices[None, :]) <= HALF).astype(jnp.float32)
    return in_window / lax.optimization_barrier(jnp.sum(in_window, axis=0, keepdims=True))

def inverse_table(seg_total):
    bins = K0 + jnp.arange(F, dtype=jnp.int32)[:, None]
    lag_index = jnp.arange(LAG_COUNT, dtype=jnp.int32)[None, :] - LAG_COUNT // 2
    angles = jnp.mod(bins * lag_index, L).astype(jnp.float32) * (2.0 * math.pi / L)
    factor = 1.0 / math.sqrt(seg_total * F)
    return (jnp.concatenate([jnp.cos(angles), -jnp.sin(angles)], axis=0) * factor).astype(jnp.bfloat16)

def whiten_segment(segment):
    spectrum = jnp.dot(segment.astype(jnp.float32).T, forward_table(), precision=lax.Precision.HIGHEST)
    real_part = spectrum[:, :F]
    imag_part = spectrum[:, F:]
    magnitude = jnp.sqrt(real_part * real_part + imag_part * imag_part)
    level = jnp.dot(magnitude, smoothing(), precision=lax.Precision.HIGHEST)
    inverse_level = 1.0 / (level + 1e-06)
    return (spectrum * jnp.concatenate([inverse_level, inverse_level], axis=1)).astype(jnp.bfloat16)

def cross_spectra(source_rows, receiver_rows):
    src_real = source_rows[:, :, None, :F].astype(jnp.float32)
    src_imag = source_rows[:, :, None, F:].astype(jnp.float32)
    rcv_real = receiver_rows[:, None, :, :F].astype(jnp.float32)
    rcv_imag = receiver_rows[:, None, :, F:].astype(jnp.float32)
    real_sum = lax.optimization_barrier(jnp.sum(src_real * rcv_real + src_imag * rcv_imag, axis=0))
    imag_sum = lax.optimization_barrier(jnp.sum(src_real * rcv_imag - src_imag * rcv_real, axis=0))
    return jnp.concatenate([real_sum, imag_sum], axis=-1).astype(jnp.bfloat16)

def reference(records, quality, tile_list, tile_slot_owner):
    white = lax.map(whiten_segment, records)
    white = white * quality.astype(jnp.bfloat16)[:, :, None]
    inverse = inverse_table(SEGS).astype(jnp.float32)
    stride = BLOCK_CHANNELS // VIRTUAL_SOURCES
    groups = SEGS // SEG_DEV

    def one_tile(tile_pair):
        source_start = (tile_pair[0] * BLOCK_CHANNELS).astype(jnp.int32)
        receiver_start = (tile_pair[1] * BLOCK_CHANNELS).astype(jnp.int32)
        source_rows = lax.dynamic_slice_in_dim(white, source_start, BLOCK_CHANNELS, 1)[:, ::stride]
        receiver_rows = lax.dynamic_slice_in_dim(white, receiver_start, BLOCK_CHANNELS, 1)
        source_rows = source_rows.reshape(groups, SEG_DEV, VIRTUAL_SOURCES, 2 * F)
        receiver_rows = receiver_rows.reshape(groups, SEG_DEV, BLOCK_CHANNELS, 2 * F)
        cross_part = jax.vmap(cross_spectra)(source_rows, receiver_rows)
        summed = lax.optimization_barrier(jnp.sum(cross_part.astype(jnp.float32), axis=0))
        product = jnp.dot(summed.reshape(VIRTUAL_SOURCES * BLOCK_CHANNELS, 2 * F), inverse, precision=lax.Precision.HIGHEST)
        return product.reshape(VIRTUAL_SOURCES, BLOCK_CHANNELS, LAG_COUNT)
    results = lax.map(one_tile, tile_list)
    correlations = jnp.zeros((SLOT_TOTAL, VIRTUAL_SOURCES, BLOCK_CHANNELS, LAG_COUNT), jnp.float32)
    return correlations.at[tile_slot_owner].set(results)
```

```python
import math

import jax
import jax.numpy as jnp
import ml_dtypes
import numpy as np
from jax import lax
from jax.experimental import pallas as pl
from jax.experimental.pallas import tpu as pltpu
from jax.sharding import PartitionSpec as P

L = 1920
F = 768
K0 = 8
HALF = 32
LAG_COUNT = 512
BLOCK = 128
SOURCES = 16
TPS = 3
REACH = 2
SEG_DEV = 4
SEGS = 16
NB = 32
TCAP = 6
TM = 4
SLAB = L // NB
ROWS = 64
PART = BLOCK // TM
SRC_PART = SOURCES // TM
MIB = 1 << 20

BF16 = jnp.bfloat16
F32 = jnp.float32


def forward_table():
    n = np.arange(L)[:, None]
    q = K0 + np.arange(F)[None, :]
    angles = (n * q % L) * (2.0 * np.pi / L)
    window = 0.5 - 0.5 * np.cos(np.arange(L) * (2.0 * np.pi / L))
    table = np.concatenate([np.cos(angles), -np.sin(angles)], axis=1) * window[:, None]
    padded = np.zeros((NB, ROWS, 2 * F))
    padded[:, :SLAB] = table.reshape(NB, SLAB, 2 * F)
    return padded.reshape(NB * ROWS, 2 * F).astype(ml_dtypes.bfloat16)


def smoothing():
    k = np.arange(F)
    inside = (np.abs(k[:, None] - k[None, :]) <= HALF).astype(np.float64)
    inverse_count = 1.0 / inside.sum(axis=0, keepdims=True)
    return inside.astype(ml_dtypes.bfloat16), inverse_count.astype(np.float32)


def inverse_table():
    q = K0 + np.arange(F)[:, None]
    lag = np.arange(LAG_COUNT)[None, :] - LAG_COUNT // 2
    angles = (q * lag % L) * (2.0 * np.pi / L)
    table = np.concatenate([np.cos(angles), -np.sin(angles)], axis=0) / math.sqrt(SEGS * F)
    return table.astype(ml_dtypes.bfloat16)


def interleave():
    order = np.zeros((SEG_DEV * BLOCK, SEG_DEV * BLOCK))
    for s in range(SEG_DEV):
        for j in range(TM):
            for c in range(PART):
                order[s * BLOCK + j * PART + c, j * BLOCK + s * PART + c] = 1.0
    return order.astype(ml_dtypes.bfloat16)


PACK_BLOCKS = 8


def pack_kernel(own, records, quality, order, spread, out):
    step = pl.program_id(0)
    marks = jnp.concatenate([quality[s : s + 1, :] for s in range(SEG_DEV)], axis=1)
    marks = jnp.broadcast_to(marks.astype(F32), (16, SEG_DEV * BLOCK)).astype(BF16)
    marks = jnp.dot(marks, order[...], preferred_element_type=F32)[:1]
    row = lax.broadcasted_iota(jnp.int32, (ROWS, SEG_DEV * BLOCK), 0)
    for k in range(PACK_BLOCKS):
        lanes = slice(k * BLOCK, (k + 1) * BLOCK)
        x = jnp.concatenate([records[s, :, lanes] for s in range(SEG_DEV)], axis=1)
        y = jnp.dot(x, order[...], preferred_element_type=F32).astype(BF16)
        y = jnp.dot(spread[...], y, preferred_element_type=F32)
        mine = step * PACK_BLOCKS + k == own[0]
        y = jnp.where((row == SLAB) & mine, marks, y).astype(BF16)
        for j in range(TM):
            out[k * TM + j] = y[:, j * BLOCK : (j + 1) * BLOCK]


def pack(own, records, quality):
    spread = np.eye(ROWS, SLAB).astype(ml_dtypes.bfloat16)
    return pl.pallas_call(
        pack_kernel,
        out_shape=jax.ShapeDtypeStruct((NB * TM, ROWS, BLOCK), BF16),
        grid_spec=pltpu.PrefetchScalarGridSpec(
            num_scalar_prefetch=1,
            grid=(NB // PACK_BLOCKS,),
            in_specs=[
                pl.BlockSpec((SEG_DEV, SLAB, PACK_BLOCKS * BLOCK), lambda g, own: (0, 0, g)),
                pl.BlockSpec((SEG_DEV, BLOCK), lambda g, own: (0, 0)),
                pl.BlockSpec((SEG_DEV * BLOCK, SEG_DEV * BLOCK), lambda g, own: (0, 0)),
                pl.BlockSpec((ROWS, SLAB), lambda g, own: (0, 0)),
            ],
            out_specs=pl.BlockSpec((PACK_BLOCKS * TM, ROWS, BLOCK), lambda g, own: (g, 0, 0)),
        ),
        compiler_params=pltpu.CompilerParams(vmem_limit_bytes=32 * MIB),
        name="pack",
    )(own, records, quality, interleave(), spread)


def whiten_kernel(own, slabs, table, inside, inverse_count, white, sources):
    marks = slabs[pl.ds(own[0], 1), 0, pl.ds(48, 16), :][0, SLAB - 48 : SLAB - 47, :]
    x = slabs[:, 0].reshape(NB * ROWS, BLOCK) * marks
    spectrum = lax.dot_general(x, table[...], (((0,), (0,)), ((), ())), preferred_element_type=F32)
    re = spectrum[:, :F]
    im = spectrum[:, F:]
    magnitude = jnp.sqrt(re * re + im * im).astype(BF16)
    level = jnp.dot(magnitude, inside[...], preferred_element_type=F32) * inverse_count[...]
    inverse_level = 1.0 / (level + 1e-6)
    for half, part in ((0, re), (1, im)):
        lanes = slice(half * F, (half + 1) * F)
        value = part * inverse_level
        white[0, :, lanes] = value.astype(BF16)
        picked = value.reshape(SEG_DEV * SRC_PART, BLOCK // SOURCES, F)[:, 0, :]
        sources[0, :, lanes] = picked.astype(BF16)


def whiten(own, slabs):
    inside, inverse_count = smoothing()
    rows = SEG_DEV * PART
    return pl.pallas_call(
        whiten_kernel,
        out_shape=(
            jax.ShapeDtypeStruct((TM, rows, 2 * F), BF16),
            jax.ShapeDtypeStruct((TM, SEG_DEV * SRC_PART, 2 * F), BF16),
        ),
        grid_spec=pltpu.PrefetchScalarGridSpec(
            num_scalar_prefetch=1,
            grid=(TM,),
            in_specs=[
                pl.BlockSpec((NB, 1, ROWS, BLOCK), lambda i, own: (0, i, 0, 0)),
                pl.BlockSpec((NB * ROWS, 2 * F), lambda i, own: (0, 0)),
                pl.BlockSpec((F, F), lambda i, own: (0, 0)),
                pl.BlockSpec((1, F), lambda i, own: (0, 0)),
            ],
            out_specs=(
                pl.BlockSpec((1, rows, 2 * F), lambda i, own: (i, 0, 0)),
                pl.BlockSpec((1, SEG_DEV * SRC_PART, 2 * F), lambda i, own: (i, 0, 0)),
            ),
        ),
        compiler_params=pltpu.CompilerParams(vmem_limit_bytes=48 * MIB),
        name="whiten",
    )(own, slabs.reshape(NB, TM, ROWS, BLOCK), forward_table(), inside, inverse_count)


LANES = 128


def tile_kernel(
    pick, s0, s1, s2, s3, inverse, r0, r1, r2, r3, r4, r5, o0, o1, o2, o3, held, src, rcv, cross, sem
):
    for index, ref in enumerate((r0, r1, r2, r3, r4, r5)):

        @pl.when(pick[0] == index)
        def _():
            pltpu.make_async_copy(ref, held, sem).start()

    for rel, ref in enumerate((s0, s1, s2, s3)):
        src[rel] = ref[...].astype(F32)
    pltpu.make_async_copy(r0, held, sem).wait()
    rcv[...] = held[...].astype(F32)
    steps = F // LANES

    def body(step, carry):
        rel = step // steps
        at = pl.multiple_of(lax.rem(step, steps) * LANES, LANES)
        re = [jnp.zeros((PART, LANES), F32)] * SRC_PART
        im = [jnp.zeros((PART, LANES), F32)] * SRC_PART
        for s in range(SEGS):
            br = rcv[s * PART : (s + 1) * PART, pl.ds(at, LANES)]
            bi = rcv[s * PART : (s + 1) * PART, pl.ds(F + at, LANES)]
            for v in range(SRC_PART):
                row = s * SRC_PART + v
                ar = src[rel, row : row + 1, pl.ds(at, LANES)]
                ai = src[rel, row : row + 1, pl.ds(F + at, LANES)]
                re[v] = re[v] + (ar * br + ai * bi)
                im[v] = im[v] + (ar * bi - ai * br)
        for v in range(SRC_PART):
            rows = slice(v * PART, (v + 1) * PART)
            cross[rel, rows, pl.ds(at, LANES)] = re[v].astype(BF16)
            cross[rel, rows, pl.ds(F + at, LANES)] = im[v].astype(BF16)
        return carry

    lax.fori_loop(0, TM * steps, body, 0)
    for rel, ref in enumerate((o0, o1, o2, o3)):
        ref[...] = jnp.dot(cross[rel], inverse[...], preferred_element_type=F32).astype(BF16)


def tile(pick, sources, inverse, receivers):
    whole = lambda: pl.BlockSpec(memory_space=pltpu.VMEM)
    rows = SRC_PART * PART
    return pl.pallas_call(
        tile_kernel,
        out_shape=[jax.ShapeDtypeStruct((rows, LAG_COUNT), BF16)] * TM,
        in_specs=[pl.BlockSpec(memory_space=pltpu.SMEM)]
        + [whole() for _ in range(TM + 1)]
        + [pl.BlockSpec(memory_space=pl.ANY)] * 6,
        out_specs=[whole() for _ in range(TM)],
        scratch_shapes=[
            pltpu.VMEM((SEGS * PART, 2 * F), BF16),
            pltpu.VMEM((TM, SEGS * SRC_PART, 2 * F), F32),
            pltpu.VMEM((SEGS * PART, 2 * F), F32),
            pltpu.VMEM((TM, rows, 2 * F), BF16),
            pltpu.SemaphoreType.DMA,
        ],
        compiler_params=pltpu.CompilerParams(vmem_limit_bytes=48 * MIB),
        cost_estimate=pl.CostEstimate(
            flops=2 * SOURCES * PART * 2 * F * LAG_COUNT, bytes_accessed=8 * MIB, transcendentals=0
        ),
        name="tile",
    )(pick, *sources, inverse, *receivers)


def gather_kernel(place, own, *refs):
    pieces, out = refs[:-1], refs[-1]
    slot = pl.program_id(0)
    for candidate in range(2 * TPS + 1):

        @pl.when(place[slot] == candidate)
        def _():
            if candidate == 2 * TPS:
                out[...] = jnp.zeros_like(out)
                return
            for rel in range(TM):
                value = pieces[candidate * TM + rel][...].astype(F32)
                at = pl.multiple_of(lax.rem(own[0] + TM - rel, TM) * PART, PART)
                out[0, :, pl.ds(at, PART), :] = value.reshape(SRC_PART, PART, LAG_COUNT)


def gather(place, own, pieces):
    rows = SRC_PART * PART
    return pl.pallas_call(
        gather_kernel,
        out_shape=jax.ShapeDtypeStruct((TCAP, SRC_PART, BLOCK, LAG_COUNT), F32),
        grid_spec=pltpu.PrefetchScalarGridSpec(
            num_scalar_prefetch=2,
            grid=(TCAP,),
            in_specs=[pl.BlockSpec((rows, LAG_COUNT), lambda s, *_: (0, 0)) for _ in pieces],
            out_specs=pl.BlockSpec((1, SRC_PART, BLOCK, LAG_COUNT), lambda s, *_: (s, 0, 0, 0)),
        ),
        compiler_params=pltpu.CompilerParams(vmem_limit_bytes=48 * MIB),
        name="gather",
    )(place, own, *pieces)


def shifted(value, axis, distance):
    count = lax.axis_size(axis)
    return lax.ppermute(value, axis, [(i, (i + distance) % count) for i in range(count)])


def per_device(records, quality, tile_list, tile_slot_owner):
    chan = lax.axis_index("chan").astype(jnp.int32)
    time = lax.axis_index("tm").astype(jnp.int32)
    own = chan.reshape(1)

    slabs = pack(own, records, quality)
    slabs = lax.all_to_all(slabs, ("chan", "tm"), split_axis=0, concat_axis=0, tiled=True)
    white, sources = whiten(own, slabs)
    white = white.reshape(SEGS * PART, 2 * F)
    sources = sources.reshape(SEGS * SRC_PART, 2 * F)
    sources = [sources] + [shifted(sources, "tm", -rel) for rel in range(1, TM)]

    below = shifted(white, "chan", 2)
    above = shifted(white, "chan", -2)
    mate = lax.ppermute(white, "chan", [(i, i ^ 1) for i in range(NB)])
    even_below = lax.ppermute(below, "chan", [(i, i - 1) for i in range(1, NB, 2)])
    odd_above = lax.ppermute(above, "chan", [(i, i + 1) for i in range(0, NB, 2)])
    receivers = [white, below, above, mate, even_below, odd_above]
    odd = lax.rem(chan, 2)

    first = chan * TPS
    mine = lax.dynamic_slice(tile_list, (first, 0), (TPS, 2))[:, 1]
    offset = jnp.mod(mine - chan + REACH, NB)
    choice = jnp.where(
        odd == 1, jnp.array([1, 3, 0, 5, 2], jnp.int32), jnp.array([1, 4, 0, 3, 2], jnp.int32)
    )
    choice = jnp.sum(
        jnp.where(offset[:, None] == jnp.arange(2 * REACH + 1)[None, :], choice[None, :], 0), axis=1
    ).astype(jnp.int32)

    home = lax.dynamic_slice(tile_slot_owner, (first,), (TPS,))
    moved = lax.dynamic_slice(tile_slot_owner, (jnp.mod(chan - 1, NB) * TPS,), (TPS,))
    named = jnp.concatenate([home, moved])
    slots = chan * TCAP + jnp.arange(TCAP, dtype=jnp.int32)
    place = 2 * TPS + jnp.sum(
        jnp.where(
            slots[:, None] == named[None, :],
            jnp.arange(2 * TPS, dtype=jnp.int32)[None, :] - 2 * TPS,
            0,
        ),
        axis=1,
    )

    inverse = inverse_table()
    stay, move = [], []
    for t in range(TPS):
        parts = tile(choice[t : t + 1], sources, inverse, receivers)
        parts = [parts[0]] + [shifted(parts[rel], "tm", rel) for rel in range(1, TM)]
        stay += parts
        move += [shifted(part, "chan", 1) for part in parts]
    return gather(place.astype(jnp.int32), time.reshape(1), stay + move)


def solution(mesh):
    placed = (P("tm", "chan", None), P("tm", "chan"), P(), P())
    return jax.shard_map(
        per_device,
        mesh=mesh,
        in_specs=placed,
        out_specs=P("chan", "tm", None, None),
        check_vma=False,
    )
```

```python
import math

import jax
import jax.numpy as jnp
import ml_dtypes
import numpy as np
from jax import lax
from jax.experimental import pallas as pl
from jax.experimental.pallas import tpu as pltpu
from jax.sharding import PartitionSpec as P

L = 1920
F = 768
K0 = 8
HALF = 32
LAG_COUNT = 512
BLOCK = 128
SOURCES = 16
TPS = 3
REACH = 2
SEG_DEV = 4
SEGS = 16
NB = 32
TCAP = 6
TM = 4
SLAB = L // NB
ROWS = 64
PART = BLOCK // TM
SRC_PART = SOURCES // TM
MIB = 1 << 20
LANES = 128
GROUP = 8
STEP = 128

BF16 = jnp.bfloat16
F32 = jnp.float32


def forward_table():
    n = np.arange(L)[None, :]
    q = K0 + np.arange(F)[:, None]
    angles = (n * q % L) * (2.0 * np.pi / L)
    window = 0.5 - 0.5 * np.cos(np.arange(L) * (2.0 * np.pi / L))
    table = np.concatenate([np.cos(angles), -np.sin(angles)], axis=0) * window[None, :]
    padded = np.zeros((2 * F, NB, ROWS))
    padded[:, :, :SLAB] = table.reshape(2 * F, NB, SLAB)
    return padded.reshape(2 * F, NB * ROWS).astype(ml_dtypes.bfloat16)


def smoothing():
    k = np.arange(F)
    inside = (np.abs(k[:, None] - k[None, :]) <= HALF).astype(np.float64)
    inverse_count = 1.0 / inside.sum(axis=1, keepdims=True)
    return inside.astype(ml_dtypes.bfloat16), inverse_count.astype(np.float32)


def inverse_table():
    q = K0 + np.arange(F)[None, :]
    lag = np.arange(LAG_COUNT)[:, None] - LAG_COUNT // 2
    angles = (q * lag % L) * (2.0 * np.pi / L)
    table = np.concatenate([np.cos(angles), -np.sin(angles)], axis=1) / math.sqrt(SEGS * F)
    return table.astype(ml_dtypes.bfloat16)


def source_lanes():
    pick = np.zeros((TM, 2, BLOCK, LANES))
    for i in range(TM):
        for half in range(2):
            for s in range(SEG_DEV):
                for v in range(SRC_PART):
                    lane = half * SRC_PART * SEGS + v * SEGS + i * SEG_DEV + s
                    pick[i, half, s * PART + v * (BLOCK // SOURCES), lane] = 1.0
    return pick.astype(ml_dtypes.bfloat16)


def spread_lanes():
    spread = np.zeros((SRC_PART, LANES, 2 * LANES))
    for v in range(SRC_PART):
        for half in range(2):
            for s in range(SEGS):
                lane = half * LANES + s * GROUP
                spread[v, half * SRC_PART * SEGS + v * SEGS + s, lane : lane + GROUP] = 1.0
    return spread.astype(ml_dtypes.bfloat16)


def tile_lanes():
    order = np.zeros((TPS * LANES, SEG_DEV * LANES))
    for t in range(TPS):
        for s in range(SEG_DEV):
            for c in range(PART):
                order[t * LANES + s * PART + c, s * LANES + t * PART + c] = 1.0
    return order.astype(ml_dtypes.bfloat16)


def interleave():
    order = np.zeros((SEG_DEV * BLOCK, SEG_DEV * BLOCK))
    for s in range(SEG_DEV):
        for j in range(TM):
            for c in range(PART):
                order[s * BLOCK + j * PART + c, j * BLOCK + s * PART + c] = 1.0
    return order.astype(ml_dtypes.bfloat16)


PACK_BLOCKS = 8


def pack_kernel(own, records, quality, order, out):
    step = pl.program_id(0)
    marks = jnp.concatenate([quality[s : s + 1, :] for s in range(SEG_DEV)], axis=1)
    marks = jnp.broadcast_to(marks.astype(F32), (16, SEG_DEV * BLOCK)).astype(BF16)
    marks = jnp.dot(marks, order[...], preferred_element_type=F32)[:1]
    row = lax.broadcasted_iota(jnp.int32, (ROWS, SEG_DEV * BLOCK), 0)
    x = jnp.concatenate(
        [
            jnp.concatenate(
                [records[s, :, k * BLOCK : (k + 1) * BLOCK] for s in range(SEG_DEV)], axis=1
            )
            for k in range(PACK_BLOCKS)
        ],
        axis=0,
    )
    y = jnp.dot(x, order[...], preferred_element_type=F32)
    for k in range(PACK_BLOCKS):
        mine = step * PACK_BLOCKS + k == own[0]
        extra = jnp.where((row == SLAB) & mine, marks, 0.0)
        block = jnp.where(row < SLAB, y[k * ROWS : (k + 1) * ROWS], extra).astype(BF16)
        for j in range(TM):
            out[k * TM + j] = block[:, j * BLOCK : (j + 1) * BLOCK]


def pack(own, records, quality):
    return pl.pallas_call(
        pack_kernel,
        out_shape=jax.ShapeDtypeStruct((NB * TM, ROWS, BLOCK), BF16),
        grid_spec=pltpu.PrefetchScalarGridSpec(
            num_scalar_prefetch=1,
            grid=(NB // PACK_BLOCKS,),
            in_specs=[
                pl.BlockSpec((SEG_DEV, ROWS, PACK_BLOCKS * BLOCK), lambda g, own: (0, 0, g)),
                pl.BlockSpec((SEG_DEV, BLOCK), lambda g, own: (0, 0)),
                pl.BlockSpec(memory_space=pltpu.VMEM),
            ],
            out_specs=pl.BlockSpec((PACK_BLOCKS * TM, ROWS, BLOCK), lambda g, own: (g, 0, 0)),
        ),
        compiler_params=pltpu.CompilerParams(vmem_limit_bytes=24 * MIB),
        name="pack",
    )(own, records, quality, interleave())


PAIR = 2


def whiten_kernel(own, slabs, table, inside, inverse_count, pick, white, sources, total):
    step = pl.program_id(0)
    lanes = []
    for i in range(PAIR):
        marks = slabs[pl.ds(own[0], 1), i, pl.ds(48, 16), :][0, SLAB - 48 : SLAB - 47, :]
        lanes.append(slabs[:, i].reshape(NB * ROWS, BLOCK) * marks)
    x = jnp.concatenate(lanes, axis=1)
    spectrum = jnp.dot(table[...], x, preferred_element_type=F32)
    re = spectrum[:F]
    im = spectrum[F:]
    magnitude = jnp.sqrt(re * re + im * im).astype(BF16)
    level = jnp.dot(inside[...], magnitude, preferred_element_type=F32) * inverse_count[...]
    inverse_level = 1.0 / (level + 1e-6)

    @pl.when(step == 0)
    def _():
        total[...] = jnp.zeros_like(total)

    for half, part in ((0, re), (1, im)):
        value = (part * inverse_level).astype(BF16)
        for i in range(PAIR):
            mine = value[:, i * BLOCK : (i + 1) * BLOCK]
            white[i, half] = mine
            total[...] += jnp.dot(mine, pick[step * PAIR + i, half], preferred_element_type=F32)
    sources[...] = total[...].astype(BF16)


def whiten(own, slabs):
    inside, inverse_count = smoothing()
    return pl.pallas_call(
        whiten_kernel,
        out_shape=(
            jax.ShapeDtypeStruct((TM, 2, F, BLOCK), BF16),
            jax.ShapeDtypeStruct((F, LANES), BF16),
        ),
        grid_spec=pltpu.PrefetchScalarGridSpec(
            num_scalar_prefetch=1,
            grid=(TM // PAIR,),
            in_specs=[pl.BlockSpec((NB, PAIR, ROWS, BLOCK), lambda i, own: (0, i, 0, 0))]
            + [pl.BlockSpec(memory_space=pltpu.VMEM)] * 4,
            out_specs=(
                pl.BlockSpec((PAIR, 2, F, BLOCK), lambda i, own: (i, 0, 0, 0)),
                pl.BlockSpec((F, LANES), lambda i, own: (0, 0)),
            ),
            scratch_shapes=[pltpu.VMEM((F, LANES), F32)],
        ),
        compiler_params=pltpu.CompilerParams(vmem_limit_bytes=28 * MIB),
        name="whiten",
    )(own, slabs.reshape(NB, TM, ROWS, BLOCK), forward_table(), inside, inverse_count, source_lanes())


def diagonal_kernel(s0, s1, s2, s3, spread, out):
    rows = STEP
    groups = rows // GROUP
    row = lax.broadcasted_iota(jnp.int32, (rows, 2 * LANES), 0)
    lane = lax.broadcasted_iota(jnp.int32, (rows, 2 * LANES), 1)
    keep = jnp.bitwise_and(row, GROUP - 1) == jnp.bitwise_and(lane, GROUP - 1)
    for rel, ref in enumerate((s0, s1, s2, s3)):
        for pair in range(SRC_PART // 2):
            same, turned = [], []
            for v in (2 * pair, 2 * pair + 1):
                wide = jnp.dot(ref[...], spread[v], preferred_element_type=F32)
                wide = jnp.where(keep, wide, 0.0)
                swap = jnp.concatenate([-wide[:, LANES:], wide[:, :LANES]], axis=1)
                same.append(wide.reshape(groups, GROUP, 2 * LANES))
                turned.append(swap.reshape(groups, GROUP, 2 * LANES))
            at = (rel * SRC_PART + 2 * pair) * GROUP
            out[:, at : at + 2 * GROUP, :] = jnp.concatenate(same, axis=1).astype(BF16)
            at += SOURCES * GROUP
            out[:, at : at + 2 * GROUP, :] = jnp.concatenate(turned, axis=1).astype(BF16)


def diagonal(sources):
    groups = STEP // GROUP
    wide = 2 * SOURCES * GROUP
    return pl.pallas_call(
        diagonal_kernel,
        out_shape=jax.ShapeDtypeStruct((F // GROUP, wide, 2 * LANES), BF16),
        grid=(F // STEP,),
        in_specs=[pl.BlockSpec((STEP, LANES), lambda g: (g, 0))] * TM
        + [pl.BlockSpec(memory_space=pltpu.VMEM)],
        out_specs=pl.BlockSpec((groups, wide, 2 * LANES), lambda g: (g, 0, 0)),
        compiler_params=pltpu.CompilerParams(vmem_limit_bytes=24 * MIB),
        cost_estimate=pl.CostEstimate(flops=1, bytes_accessed=1, transcendentals=0),
        name="diagonal",
    )(*sources, spread_lanes())


def cross_kernel(pick, diag, order, *refs):
    receivers, (out, held, wide, sem) = refs[:6], refs[6:]
    step = pl.program_id(0)
    steps = F // STEP

    def copy(ref, t, k):
        rows = pl.ds(k * STEP, STEP)
        return pltpu.make_async_copy(
            ref.at[:, :, rows, :], held.at[k, t], sem.at[k, t]
        )

    @pl.when(step == 0)
    def _():
        for k in range(steps):
            for t in range(TPS):
                for index, ref in enumerate(receivers):

                    @pl.when(pick[t] == index)
                    def _():
                        copy(ref, t, k).start()

    for t in range(TPS):
        copy(receivers[0], t, step).wait()
    x = jnp.concatenate(
        [held[step, t].reshape(TM * 2 * STEP, LANES) for t in range(TPS)], axis=1
    )
    y = jnp.dot(x, order[...], preferred_element_type=F32)
    for i in range(TM):
        for half in range(2):
            at = (i * 2 + half) * STEP
            for s in range(SEG_DEV):
                wide[half * SEGS + i * SEG_DEV + s] = y[
                    at : at + STEP, s * LANES : (s + 1) * LANES
                ]

    def group(pair, carry):
        outs = []
        for g in range(2):
            at = pl.multiple_of((pair * 2 + g) * GROUP, GROUP)
            b = wide[:, pl.ds(at, GROUP), :].reshape(2 * SEGS * GROUP, LANES).astype(BF16)
            outs.append(jnp.dot(diag[pair * 2 + g], b, preferred_element_type=F32))
        both = jnp.concatenate(
            [o.reshape(2 * SOURCES, GROUP, LANES) for o in outs], axis=1
        ).astype(BF16)
        rows = pl.ds(pl.multiple_of(pair * 2 * GROUP, 2 * GROUP), 2 * GROUP)
        out[:, 0, rows, :] = both[:SOURCES]
        out[:, 1, rows, :] = both[SOURCES:]
        return carry

    lax.fori_loop(0, STEP // (2 * GROUP), group, 0, unroll=2)


def cross(pick, diag, receivers):
    groups = STEP // GROUP
    wide = 2 * SOURCES * GROUP
    return pl.pallas_call(
        cross_kernel,
        out_shape=jax.ShapeDtypeStruct((SOURCES, 2, F, LANES), BF16),
        grid_spec=pltpu.PrefetchScalarGridSpec(
            num_scalar_prefetch=1,
            grid=(F // STEP,),
            in_specs=[
                pl.BlockSpec((groups, wide, 2 * LANES), lambda g, *_: (g, 0, 0)),
                pl.BlockSpec(memory_space=pltpu.VMEM),
            ]
            + [pl.BlockSpec(memory_space=pl.ANY)] * 6,
            out_specs=pl.BlockSpec((SOURCES, 2, STEP, LANES), lambda g, *_: (0, 0, g, 0)),
            scratch_shapes=[
                pltpu.VMEM((F // STEP, TPS, TM, 2, STEP, LANES), BF16),
                pltpu.VMEM((2 * SEGS, STEP, LANES), F32),
                pltpu.SemaphoreType.DMA((F // STEP, TPS)),
            ],
        ),
        compiler_params=pltpu.CompilerParams(vmem_limit_bytes=32 * MIB),
        cost_estimate=pl.CostEstimate(flops=1, bytes_accessed=1, transcendentals=0),
        name="cross",
    )(pick, diag, tile_lanes(), *receivers)


def stack_kernel(spectra, inverse, out):
    for pair in range(SRC_PART // 2):
        x = jnp.concatenate(
            [spectra[2 * pair + v].reshape(2 * F, LANES) for v in range(2)], axis=1
        )
        y = jnp.dot(inverse[...], x, preferred_element_type=F32)
        for v in range(2):
            value = y[:, v * LANES : (v + 1) * LANES].T.astype(BF16)
            for t in range(TPS):
                at = (t * SRC_PART + 2 * pair + v) * PART
                out[at : at + PART, :] = value[t * PART : (t + 1) * PART, :]


def stack(spectra, rel, inverse):
    rows = TPS * SRC_PART * PART
    return pl.pallas_call(
        stack_kernel,
        out_shape=jax.ShapeDtypeStruct((rows, LAG_COUNT), BF16),
        grid=(1,),
        in_specs=[
            pl.BlockSpec((SRC_PART, 2, F, LANES), lambda g: (rel, 0, 0, 0)),
            pl.BlockSpec(memory_space=pltpu.VMEM),
        ],
        out_specs=pl.BlockSpec((rows, LAG_COUNT), lambda g: (0, 0)),
        compiler_params=pltpu.CompilerParams(vmem_limit_bytes=24 * MIB),
        cost_estimate=pl.CostEstimate(flops=1, bytes_accessed=1, transcendentals=0),
        name="stack",
    )(spectra, inverse)


def gather_kernel(place, own, *refs):
    pieces, out = refs[:-1], refs[-1]
    slot = pl.program_id(0)
    rows = SRC_PART * PART
    for candidate in range(2 * TPS + 1):

        @pl.when(place[slot] == candidate)
        def _():
            if candidate == 2 * TPS:
                out[...] = jnp.zeros_like(out)
                return
            moved, t = divmod(candidate, TPS)
            for rel in range(TM):
                value = pieces[moved * TM + rel][t * rows : (t + 1) * rows, :].astype(F32)
                at = pl.multiple_of(lax.rem(own[0] + TM - rel, TM) * PART, PART)
                out[0, :, pl.ds(at, PART), :] = value.reshape(SRC_PART, PART, LAG_COUNT)


def gather(place, own, pieces):
    return pl.pallas_call(
        gather_kernel,
        out_shape=jax.ShapeDtypeStruct((TCAP, SRC_PART, BLOCK, LAG_COUNT), F32),
        grid_spec=pltpu.PrefetchScalarGridSpec(
            num_scalar_prefetch=2,
            grid=(TCAP,),
            in_specs=[pl.BlockSpec(memory_space=pltpu.VMEM) for _ in pieces],
            out_specs=pl.BlockSpec((1, SRC_PART, BLOCK, LAG_COUNT), lambda s, *_: (s, 0, 0, 0)),
        ),
        compiler_params=pltpu.CompilerParams(vmem_limit_bytes=24 * MIB),
        name="gather",
    )(place, own, *pieces)


def shifted(value, axis, distance):
    count = lax.axis_size(axis)
    return lax.ppermute(value, axis, [(i, (i + distance) % count) for i in range(count)])


def on_chip(below, above):
    return [
        lax.ppermute(below, "chan", [(i, i - 1) for i in range(1, NB, 2)]),
        lax.ppermute(above, "chan", [(i, i + 1) for i in range(0, NB, 2)]),
    ]


def per_device(records, quality, tile_list, tile_slot_owner):
    chan = lax.axis_index("chan").astype(jnp.int32)
    time = lax.axis_index("tm").astype(jnp.int32)
    own = chan.reshape(1)

    slabs = pack(own, records, quality)
    slabs = lax.all_to_all(slabs, ("chan", "tm"), split_axis=0, concat_axis=0, tiled=True)
    white, sources = whiten(own, slabs)
    sources = [sources] + [shifted(sources, "tm", -rel) for rel in range(1, TM)]
    diag = diagonal(sources)
    below = shifted(white, "chan", 2)
    above = shifted(white, "chan", -2)
    mate = lax.ppermute(white, "chan", [(i, i ^ 1) for i in range(NB)])
    below, above, diag = lax.optimization_barrier((below, above, diag))
    receivers = [white, below, above, mate] + on_chip(below, above)
    odd = lax.rem(chan, 2)

    first = chan * TPS
    mine = lax.dynamic_slice(tile_list, (first, 0), (TPS, 2))[:, 1]
    offset = jnp.mod(mine - chan + REACH, NB)
    choice = jnp.where(
        odd == 1, jnp.array([1, 3, 0, 5, 2], jnp.int32), jnp.array([1, 4, 0, 3, 2], jnp.int32)
    )
    choice = jnp.sum(
        jnp.where(offset[:, None] == jnp.arange(2 * REACH + 1)[None, :], choice[None, :], 0), axis=1
    ).astype(jnp.int32)

    home = lax.dynamic_slice(tile_slot_owner, (first,), (TPS,))
    moved = lax.dynamic_slice(tile_slot_owner, (jnp.mod(chan - 1, NB) * TPS,), (TPS,))
    named = jnp.concatenate([home, moved])
    slots = chan * TCAP + jnp.arange(TCAP, dtype=jnp.int32)
    place = 2 * TPS + jnp.sum(
        jnp.where(
            slots[:, None] == named[None, :],
            jnp.arange(2 * TPS, dtype=jnp.int32)[None, :] - 2 * TPS,
            0,
        ),
        axis=1,
    )

    inverse = inverse_table()
    spectra = cross(choice, diag, receivers)
    stay, move = [None] * TM, [None] * TM
    for rel in (2, 0, 1, 3):
        part = stack(spectra, rel, inverse)
        stay[rel] = shifted(part, "tm", rel) if rel else part
        move[rel] = shifted(stay[rel], "chan", 1)
    return gather(place.astype(jnp.int32), time.reshape(1), stay + move)


def solution(mesh):
    placed = (P("tm", "chan", None), P("tm", "chan"), P(), P())
    return jax.shard_map(
        per_device,
        mesh=mesh,
        in_specs=placed,
        out_specs=P("chan", "tm", None, None),
        check_vma=False,
    )
```

```python
import functools
import math

import jax
import jax.numpy as jnp
import ml_dtypes
import numpy as np
from jax import lax
from jax.experimental import pallas as pl
from jax.experimental.pallas import tpu as pltpu
from jax.sharding import PartitionSpec as P

L = 1920
F = 768
K0 = 8
HALF = 32
LAG_COUNT = 512
BLOCK = 128
SOURCES = 16
TPS = 3
REACH = 2
SEG_DEV = 4
SEGS = 16
NB = 32
TCAP = 6
TM = 4
SLAB = L // NB
ROWS = 64
PART = BLOCK // TM
SRC_PART = SOURCES // TM
MIB = 1 << 20
LANES = 128
GROUP = 8
STEP = 128
HALF_PART = PART // 2

BF16 = jnp.bfloat16
F32 = jnp.float32


def forward_table():
    n = np.arange(L)[None, :]
    q = K0 + np.arange(F)[:, None]
    angles = (n * q % L) * (2.0 * np.pi / L)
    window = 0.5 - 0.5 * np.cos(np.arange(L) * (2.0 * np.pi / L))
    table = np.concatenate([np.cos(angles), -np.sin(angles)], axis=0) * window[None, :]
    padded = np.zeros((2 * F, NB, ROWS))
    padded[:, :, :SLAB] = table.reshape(2 * F, NB, SLAB)
    return padded.reshape(2 * F, NB * ROWS).astype(ml_dtypes.bfloat16)


def smoothing():
    k = np.arange(F)
    inside = (np.abs(k[:, None] - k[None, :]) <= HALF).astype(np.float64)
    inverse_count = 1.0 / inside.sum(axis=1, keepdims=True)
    return inside.astype(ml_dtypes.bfloat16), inverse_count.astype(np.float32)


def inverse_table():
    q = K0 + np.arange(F)[None, :]
    lag = np.arange(LAG_COUNT)[:, None] - LAG_COUNT // 2
    angles = (q * lag % L) * (2.0 * np.pi / L)
    table = np.concatenate([np.cos(angles), -np.sin(angles)], axis=1) / math.sqrt(SEGS * F)
    return table.astype(ml_dtypes.bfloat16)


PAIR = 2
PARTS = TM // PAIR


def source_lanes():
    pick = np.zeros((TM, 2, BLOCK, LANES))
    for i in range(TM):
        for half in range(2):
            for s in range(SEG_DEV):
                for v in range(SRC_PART):
                    part, at = divmod(v * (BLOCK // SOURCES), HALF_PART)
                    lane = half * SRC_PART * SEGS + v * SEGS + i * SEG_DEV + s
                    pick[i, half, (part * SEG_DEV + s) * HALF_PART + at, lane] = 1.0
    return pick.astype(ml_dtypes.bfloat16)


def spread_lanes():
    spread = np.zeros((SRC_PART, LANES, 2 * LANES))
    for v in range(SRC_PART):
        for half in range(2):
            for s in range(SEGS):
                lane = half * LANES + s * GROUP
                spread[v, half * SRC_PART * SEGS + v * SEGS + s, lane : lane + GROUP] = 1.0
    return spread.astype(ml_dtypes.bfloat16)


def tile_lanes():
    count = PAIR * SEG_DEV
    order = np.zeros((TPS * LANES, count * LANES))
    for t in range(TPS):
        for s in range(count):
            for c in range(HALF_PART):
                for twin in range(2):
                    lane = s * LANES + twin * (LANES // 2) + t * HALF_PART + c
                    order[t * LANES + s * HALF_PART + c, lane] = 1.0
    return order.astype(ml_dtypes.bfloat16)


def interleave():
    order = np.zeros((SEG_DEV * BLOCK, SEG_DEV * BLOCK))
    for s in range(SEG_DEV):
        for j in range(TM):
            for c in range(PART):
                part, at = divmod(c, HALF_PART)
                lane = j * BLOCK + (part * SEG_DEV + s) * HALF_PART + at
                order[s * BLOCK + j * PART + c, lane] = 1.0
    return order.astype(ml_dtypes.bfloat16)


PACK_BLOCKS = 8


def pack_kernel(own, records, quality, order, out):
    step = pl.program_id(0)
    marks = jnp.concatenate([quality[s : s + 1, :] for s in range(SEG_DEV)], axis=1)
    marks = jnp.broadcast_to(marks.astype(F32), (16, SEG_DEV * BLOCK)).astype(BF16)
    marks = jnp.dot(marks, order[...], preferred_element_type=F32)[:1]
    row = lax.broadcasted_iota(jnp.int32, (ROWS, SEG_DEV * BLOCK), 0)
    x = jnp.concatenate(
        [
            jnp.concatenate(
                [records[s, :, k * BLOCK : (k + 1) * BLOCK] for s in range(SEG_DEV)], axis=1
            )
            for k in range(PACK_BLOCKS)
        ],
        axis=0,
    )
    y = jnp.dot(x, order[...], preferred_element_type=F32)
    for k in range(PACK_BLOCKS):
        mine = step * PACK_BLOCKS + k == own[0]
        extra = jnp.where((row == SLAB) & mine, marks, 0.0)
        block = jnp.where(row < SLAB, y[k * ROWS : (k + 1) * ROWS], extra).astype(BF16)
        for j in range(TM):
            out[k * TM + j] = block[:, j * BLOCK : (j + 1) * BLOCK]


def pack(own, records, quality):
    return pl.pallas_call(
        pack_kernel,
        out_shape=jax.ShapeDtypeStruct((NB * TM, ROWS, BLOCK), BF16),
        grid_spec=pltpu.PrefetchScalarGridSpec(
            num_scalar_prefetch=1,
            grid=(NB // PACK_BLOCKS,),
            in_specs=[
                pl.BlockSpec((SEG_DEV, ROWS, PACK_BLOCKS * BLOCK), lambda g, own: (0, 0, g)),
                pl.BlockSpec((SEG_DEV, BLOCK), lambda g, own: (0, 0)),
                pl.BlockSpec(memory_space=pltpu.VMEM),
            ],
            out_specs=pl.BlockSpec((PACK_BLOCKS * TM, ROWS, BLOCK), lambda g, own: (g, 0, 0)),
        ),
        compiler_params=pltpu.CompilerParams(vmem_limit_bytes=20 * MIB),
        name="pack",
    )(own, records, quality, interleave())


def whiten_kernel(own, slabs, table, inside, inverse_count, pick, low, high, sources, total):
    step = pl.program_id(0)
    lanes = []
    for i in range(PAIR):
        marks = slabs[pl.ds(own[0], 1), i, pl.ds(48, 16), :][0, SLAB - 48 : SLAB - 47, :]
        lanes.append(slabs[:, i].reshape(NB * ROWS, BLOCK) * marks)
    x = jnp.concatenate(lanes, axis=1)
    spectrum = jnp.dot(table[...], x, preferred_element_type=F32)
    re = spectrum[:F]
    im = spectrum[F:]
    magnitude = jnp.sqrt(re * re + im * im).astype(BF16)
    level = jnp.dot(inside[...], magnitude, preferred_element_type=F32) * inverse_count[...]
    inverse_level = 1.0 / (level + 1e-6)

    @pl.when(step == 0)
    def _():
        total[...] = jnp.zeros_like(total)

    first = lax.broadcasted_iota(jnp.int32, (F, LANES), 1) < LANES // 2
    for half, part in ((0, re), (1, im)):
        value = part * inverse_level
        pair = [value[:, i * BLOCK : (i + 1) * BLOCK] for i in range(PAIR)]
        turned = [pltpu.roll(one, LANES // 2, 1) for one in pair]
        low[0, half] = jnp.where(first, pair[0], turned[1]).astype(BF16)
        high[0, half] = jnp.where(first, turned[0], pair[1]).astype(BF16)
        for i in range(PAIR):
            total[...] += jnp.dot(
                pair[i].astype(BF16), pick[step * PAIR + i, half], preferred_element_type=F32
            )
    sources[...] = total[...].astype(BF16)


def whiten(own, slabs):
    inside, inverse_count = smoothing()
    shape = jax.ShapeDtypeStruct((TM // PAIR, 2, F, LANES), BF16)
    spec = pl.BlockSpec((1, 2, F, LANES), lambda i, own: (i, 0, 0, 0))
    return pl.pallas_call(
        whiten_kernel,
        out_shape=(shape, shape, jax.ShapeDtypeStruct((F, LANES), BF16)),
        grid_spec=pltpu.PrefetchScalarGridSpec(
            num_scalar_prefetch=1,
            grid=(TM // PAIR,),
            in_specs=[pl.BlockSpec((NB, PAIR, ROWS, BLOCK), lambda i, own: (0, i, 0, 0))]
            + [pl.BlockSpec(memory_space=pltpu.VMEM)] * 4,
            out_specs=(spec, spec, pl.BlockSpec((F, LANES), lambda i, own: (0, 0))),
            scratch_shapes=[pltpu.VMEM((F, LANES), F32)],
        ),
        compiler_params=pltpu.CompilerParams(vmem_limit_bytes=20 * MIB),
        name="whiten",
    )(own, slabs.reshape(NB, TM, ROWS, BLOCK), forward_table(), inside, inverse_count, source_lanes())


def choose_kernel(chan, below, above, out, sem):
    odd = lax.rem(chan[0], 2)

    @pl.when(odd == 1)
    def _():
        pltpu.make_async_copy(below, out, sem).start()

    @pl.when(odd == 0)
    def _():
        pltpu.make_async_copy(above, out, sem).start()

    pltpu.make_async_copy(below, out, sem).wait()


def choose(chan, below, above):
    return pl.pallas_call(
        choose_kernel,
        out_shape=jax.ShapeDtypeStruct(below.shape, below.dtype),
        in_specs=[pl.BlockSpec(memory_space=pltpu.SMEM)]
        + [pl.BlockSpec(memory_space=pl.ANY)] * 2,
        out_specs=pl.BlockSpec(memory_space=pl.ANY),
        scratch_shapes=[pltpu.SemaphoreType.DMA],
        compiler_params=pltpu.CompilerParams(vmem_limit_bytes=MIB),
        cost_estimate=pl.CostEstimate(flops=1, bytes_accessed=1, transcendentals=0),
        name="choose",
    )(chan, below, above)


def diagonal_kernel(s0, s1, s2, s3, spread, out):
    rows = STEP
    groups = rows // GROUP
    place = pl.ds(pl.program_id(0) * groups, groups)
    row = lax.broadcasted_iota(jnp.int32, (rows, 2 * LANES), 0)
    lane = lax.broadcasted_iota(jnp.int32, (rows, 2 * LANES), 1)
    keep = jnp.bitwise_and(row, GROUP - 1) == jnp.bitwise_and(lane, GROUP - 1)
    for rel, ref in enumerate((s0, s1, s2, s3)):
        for pair in range(SRC_PART // 2):
            same, turned = [], []
            for v in (2 * pair, 2 * pair + 1):
                wide = jnp.dot(ref[...], spread[v], preferred_element_type=F32)
                wide = jnp.where(keep, wide, 0.0)
                swap = jnp.concatenate([-wide[:, LANES:], wide[:, :LANES]], axis=1)
                same.append(wide.reshape(groups, GROUP, 2 * LANES))
                turned.append(swap.reshape(groups, GROUP, 2 * LANES))
            at = (rel * SRC_PART + 2 * pair) * GROUP
            out[place, at : at + 2 * GROUP, :] = jnp.concatenate(same, axis=1).astype(BF16)
            at += SOURCES * GROUP
            out[place, at : at + 2 * GROUP, :] = jnp.concatenate(turned, axis=1).astype(BF16)


def diagonal(sources):
    wide = 2 * SOURCES * GROUP
    return pl.pallas_call(
        diagonal_kernel,
        out_shape=jax.ShapeDtypeStruct((F // GROUP, wide, 2 * LANES), BF16),
        grid=(F // STEP,),
        in_specs=[pl.BlockSpec((STEP, LANES), lambda g: (g, 0))] * TM
        + [pl.BlockSpec(memory_space=pltpu.VMEM)],
        out_specs=pl.BlockSpec(memory_space=pltpu.VMEM),
        compiler_params=pltpu.CompilerParams(vmem_limit_bytes=20 * MIB),
        cost_estimate=pl.CostEstimate(flops=1, bytes_accessed=1, transcendentals=0),
        name="diagonal",
    )(*sources, spread_lanes())


RECEIVERS = 2 * REACH + 1


def chosen(chan, tiles, t):
    offset = lax.rem(tiles[1, chan * TPS + t] - chan + REACH + NB, NB)
    mate = jnp.where(lax.rem(chan, 2) == 1, 1, 3)
    near = jnp.where(offset == REACH, 0, jnp.where(offset == mate, 3, 4))
    return jnp.where(offset == 0, 1, jnp.where(offset == 2 * REACH, 2, near))


def cross_kernel(chan, tiles, diag, order, *refs):
    receivers, (out, held, wide, sem) = refs[:RECEIVERS], refs[RECEIVERS:]
    step = pl.program_id(0)
    steps = F // STEP

    def copy(ref, t, k):
        rows = pl.ds(k * STEP, STEP)
        return pltpu.make_async_copy(ref.at[:, :, rows, :], held.at[k, t], sem.at[k, t])

    @pl.when(step == 0)
    def _():
        picks = [chosen(chan[0], tiles, t) for t in range(TPS)]
        for k in range(steps):
            for t in range(TPS):
                for index, ref in enumerate(receivers):

                    @pl.when(picks[t] == index)
                    def _():
                        copy(ref, t, k).start()

    for t in range(TPS):
        copy(receivers[0], t, step).wait()
    x = jnp.concatenate(
        [held[step, t].reshape(TM // PAIR * 2 * STEP, LANES) for t in range(TPS)], axis=1
    )
    y = jnp.dot(x, order[...], preferred_element_type=F32)
    count = PAIR * SEG_DEV
    for i in range(TM // PAIR):
        for half in range(2):
            at = (i * 2 + half) * STEP
            for s in range(count):
                wide[half * SEGS + i * count + s] = y[at : at + STEP, s * LANES : (s + 1) * LANES]
    first = lax.broadcasted_iota(jnp.int32, (1, GROUP, LANES), 2) < LANES // 2

    def group(pair, carry):
        outs = []
        for g in range(2):
            at = pl.multiple_of((pair * 2 + g) * GROUP, GROUP)
            b = wide[:, pl.ds(at, GROUP), :].reshape(2 * SEGS * GROUP, LANES).astype(BF16)
            o = jnp.dot(diag[step * (STEP // GROUP) + pair * 2 + g], b, preferred_element_type=F32)
            o = o.reshape(SOURCES, 2, GROUP, LANES)
            outs.append(jnp.where(first, o[:, 0], o[:, 1]))
        both = jnp.concatenate(outs, axis=1).astype(BF16)
        rows = pl.ds(pl.multiple_of(step * STEP + pair * 2 * GROUP, 2 * GROUP), 2 * GROUP)
        out[:, 0, rows, :] = both[: SOURCES // 2]
        out[:, 1, rows, :] = both[SOURCES // 2 :]
        return carry

    lax.fori_loop(0, STEP // (2 * GROUP), group, 0, unroll=UNROLL)


UNROLL = 8


def cross(chan, tiles, diag, receivers):
    return pl.pallas_call(
        cross_kernel,
        out_shape=jax.ShapeDtypeStruct((SOURCES // 2, 2, F, LANES), BF16),
        grid_spec=pltpu.PrefetchScalarGridSpec(
            num_scalar_prefetch=2,
            grid=(F // STEP,),
            in_specs=[pl.BlockSpec(memory_space=pltpu.VMEM)] * 2
            + [pl.BlockSpec(memory_space=pl.ANY)] * RECEIVERS,
            out_specs=pl.BlockSpec(memory_space=pltpu.VMEM),
            scratch_shapes=[
                pltpu.VMEM((F // STEP, TPS, TM // PAIR, 2, STEP, LANES), BF16),
                pltpu.VMEM((2 * SEGS, STEP, LANES), F32),
                pltpu.SemaphoreType.DMA((F // STEP, TPS)),
            ],
        ),
        compiler_params=pltpu.CompilerParams(vmem_limit_bytes=20 * MIB),
        cost_estimate=pl.CostEstimate(flops=1, bytes_accessed=1, transcendentals=0),
        name="cross",
    )(chan, tiles, diag, tile_lanes(), *receivers)


def stack_kernel(rel, spectra, inverse, out):
    first = rel * SRC_PART // 2
    x = jnp.concatenate(
        [spectra[first + pair].reshape(2 * F, LANES) for pair in range(SRC_PART // 2)], axis=1
    )
    y = jnp.dot(inverse[...], x, preferred_element_type=F32)
    for pair in range(SRC_PART // 2):
        value = y[:, pair * LANES : (pair + 1) * LANES].T.astype(BF16)
        for v in range(2):
            for t in range(TPS):
                at = (t * SRC_PART + 2 * pair + v) * HALF_PART
                row = v * (LANES // 2) + t * HALF_PART
                out[at : at + HALF_PART, :] = value[row : row + HALF_PART, :]


def stack(spectra, rel, inverse):
    rows = TPS * SRC_PART * HALF_PART
    return pl.pallas_call(
        functools.partial(stack_kernel, rel),
        out_shape=jax.ShapeDtypeStruct((rows, LAG_COUNT), BF16),
        in_specs=[pl.BlockSpec(memory_space=pltpu.VMEM)] * 2,
        out_specs=pl.BlockSpec(memory_space=pltpu.VMEM),
        compiler_params=pltpu.CompilerParams(vmem_limit_bytes=10 * MIB),
        cost_estimate=pl.CostEstimate(flops=1, bytes_accessed=1, transcendentals=0),
        name="stack",
    )(spectra, inverse)


def arrange(time, pieces, t):
    rows = SRC_PART * HALF_PART
    for index, ref in enumerate(pieces):
        half, rel = divmod(index, TM)
        value = ref[t * rows : (t + 1) * rows, :].astype(F32)
        at = lax.rem(time + TM - rel, TM) * PART + half * HALF_PART
        yield pl.multiple_of(at, HALF_PART), value.reshape(SRC_PART, HALF_PART, LAG_COUNT)


def home_kernel(owners, chan, time, *refs):
    pieces, out = refs[:-1], refs[-1]
    slot = pl.program_id(0)
    out[...] = jnp.zeros_like(out)
    for t in range(TPS):

        @pl.when(owners[chan[0] * TPS + t] == chan[0] * TCAP + slot)
        def _():
            for at, value in arrange(time[0], pieces, t):
                out[0, :, pl.ds(at, HALF_PART), :] = value


def home(owners, chan, time, pieces):
    return pl.pallas_call(
        home_kernel,
        out_shape=jax.ShapeDtypeStruct((TCAP, SRC_PART, BLOCK, LAG_COUNT), F32),
        grid_spec=pltpu.PrefetchScalarGridSpec(
            num_scalar_prefetch=3,
            grid=(TCAP,),
            in_specs=[pl.BlockSpec(memory_space=pltpu.VMEM) for _ in pieces],
            out_specs=pl.BlockSpec((1, SRC_PART, BLOCK, LAG_COUNT), lambda s, *_: (s, 0, 0, 0)),
        ),
        compiler_params=pltpu.CompilerParams(vmem_limit_bytes=10 * MIB),
        cost_estimate=pl.CostEstimate(flops=1, bytes_accessed=1, transcendentals=0),
        name="home",
    )(owners, chan, time, *pieces)


def moved_kernel(owners, chan, time, *refs):
    pieces, (_, out, held, sem) = refs[:-4], refs[-4:]
    source = lax.rem(chan[0] + NB - 1, NB)
    copies = []
    for t in range(TPS):
        slot = owners[source * TPS + t] - chan[0] * TCAP
        mine = (slot >= 0) & (slot < TCAP)
        copy = pltpu.make_async_copy(held.at[t], out.at[jnp.clip(slot, 0, TCAP - 1)], sem.at[t])
        copies.append((mine, copy))

        @pl.when(mine)
        def _():
            for at, value in arrange(time[0], pieces, t):
                held[t, :, pl.ds(at, HALF_PART), :] = value
            copy.start()

    for mine, copy in copies:

        @pl.when(mine)
        def _():
            copy.wait()


def moved(owners, chan, time, pieces, result):
    return pl.pallas_call(
        moved_kernel,
        out_shape=jax.ShapeDtypeStruct(result.shape, result.dtype),
        in_specs=[pl.BlockSpec(memory_space=pltpu.SMEM)] * 3
        + [pl.BlockSpec(memory_space=pltpu.VMEM) for _ in pieces]
        + [pl.BlockSpec(memory_space=pl.ANY)],
        out_specs=pl.BlockSpec(memory_space=pl.ANY),
        scratch_shapes=[
            pltpu.VMEM((TPS, SRC_PART, BLOCK, LAG_COUNT), F32),
            pltpu.SemaphoreType.DMA((TPS,)),
        ],
        input_output_aliases={3 + len(pieces): 0},
        compiler_params=pltpu.CompilerParams(vmem_limit_bytes=12 * MIB),
        cost_estimate=pl.CostEstimate(flops=1, bytes_accessed=1, transcendentals=0),
        name="moved",
    )(owners, chan, time, *pieces, result)


def shifted(value, axis, distance):
    count = lax.axis_size(axis)
    return lax.ppermute(value, axis, [(i, (i + distance) % count) for i in range(count)])


def per_device(records, quality, tile_list, tile_slot_owner):
    chan = lax.axis_index("chan").astype(jnp.int32).reshape(1)
    time = lax.axis_index("tm").astype(jnp.int32).reshape(1)
    tiles = tile_list.T
    swap = [(i, i ^ 1) for i in range(NB)]

    slabs = pack(chan, records, quality)
    slabs = lax.all_to_all(slabs, ("chan", "tm"), split_axis=0, concat_axis=0, tiled=True)
    low, high, sources = whiten(chan, slabs)
    sources = [sources] + [shifted(sources, "tm", -rel) for rel in range(1, TM)]
    diag = diagonal(sources)

    def halo(white):
        mate = lax.ppermute(white, "chan", swap)
        return [white, shifted(white, "chan", 2), shifted(white, "chan", -2), mate]

    def complete(blocks):
        other = choose(chan, blocks[1], blocks[2])
        return blocks + [lax.ppermute(other, "chan", swap)]

    inverse = inverse_table()
    order = (2, 0, 1, 3)
    low = halo(low)
    high, low[3] = lax.optimization_barrier((high, low[3]))
    high = halo(high)
    low, diag = lax.optimization_barrier((low, diag))
    spectra = cross(chan, tiles, diag, complete(low))
    parts = [stack(spectra, rel, inverse) for rel in range(TM)]
    stay_low = [shifted(part, "tm", rel) if rel else part for rel, part in enumerate(parts)]
    high, stay_low = lax.optimization_barrier((high, stay_low))
    high = complete(high)
    move_low = [shifted(part, "chan", 1) for part in stay_low]
    spectra = cross(chan, tiles, diag, high)
    stay_high, move_high = [None] * TM, [None] * TM
    for rel in order:
        part = stack(spectra, rel, inverse)
        if rel == 0:
            part, move_low = lax.optimization_barrier((part, move_low))
        stay_high[rel] = shifted(part, "tm", rel) if rel else part
        move_high[rel] = shifted(stay_high[rel], "chan", 1)
    result = home(tile_slot_owner, chan, time, stay_low + stay_high)
    return moved(tile_slot_owner, chan, time, move_low + move_high, result)


def solution(mesh):
    placed = (P("tm", "chan", None), P("tm", "chan"), P(), P())
    return jax.shard_map(
        per_device,
        mesh=mesh,
        in_specs=placed,
        out_specs=P("chan", "tm", None, None),
        check_vma=False,
    )
```

```python
import functools
import math

import jax
import jax.numpy as jnp
import ml_dtypes
import numpy as np
from jax import lax
from jax.experimental import pallas as pl
from jax.experimental.pallas import tpu as pltpu
from jax.sharding import PartitionSpec as P

L = 1920
F = 768
K0 = 8
HALF = 32
LAG_COUNT = 512
BLOCK = 128
SOURCES = 16
TPS = 3
REACH = 2
SEG_DEV = 4
SEGS = 16
NB = 32
TCAP = 6
TM = 4
SLAB = L // NB
ROWS = 64
PART = BLOCK // TM
SRC_PART = SOURCES // TM
MIB = 1 << 20
LANES = 128
GROUP = 8
STEP = 128
HALF_PART = PART // 2

BF16 = jnp.bfloat16
F32 = jnp.float32


def forward_table():
    n = np.arange(L)[None, :]
    q = K0 + np.arange(F)[:, None]
    angles = (n * q % L) * (2.0 * np.pi / L)
    window = 0.5 - 0.5 * np.cos(np.arange(L) * (2.0 * np.pi / L))
    table = np.concatenate([np.cos(angles), -np.sin(angles)], axis=0) * window[None, :]
    padded = np.zeros((2 * F, NB, ROWS))
    padded[:, :, :SLAB] = table.reshape(2 * F, NB, SLAB)
    return padded.reshape(2 * F, NB * ROWS).astype(ml_dtypes.bfloat16)


def smoothing():
    k = np.arange(F)
    inside = (np.abs(k[:, None] - k[None, :]) <= HALF).astype(np.float64)
    inverse_count = 1.0 / inside.sum(axis=1, keepdims=True)
    return inside.astype(ml_dtypes.bfloat16), inverse_count.astype(np.float32)


def inverse_table():
    q = K0 + np.arange(F)[None, :]
    lag = np.arange(LAG_COUNT)[:, None] - LAG_COUNT // 2
    angles = (q * lag % L) * (2.0 * np.pi / L)
    table = np.concatenate([np.cos(angles), -np.sin(angles)], axis=1) / math.sqrt(SEGS * F)
    return table.astype(ml_dtypes.bfloat16)


PAIR = 2
PARTS = TM // PAIR


def source_lanes():
    pick = np.zeros((TM, 2, BLOCK, LANES))
    for i in range(TM):
        for half in range(2):
            for s in range(SEG_DEV):
                for v in range(SRC_PART):
                    part, at = divmod(v * (BLOCK // SOURCES), HALF_PART)
                    lane = half * SRC_PART * SEGS + v * SEGS + i * SEG_DEV + s
                    pick[i, half, (part * SEG_DEV + s) * HALF_PART + at, lane] = 1.0
    return pick.astype(ml_dtypes.bfloat16)


def spread_lanes():
    spread = np.zeros((SRC_PART, LANES, 2 * LANES))
    for v in range(SRC_PART):
        for half in range(2):
            for s in range(SEGS):
                lane = half * LANES + s * GROUP
                spread[v, half * SRC_PART * SEGS + v * SEGS + s, lane : lane + GROUP] = 1.0
    return spread.astype(ml_dtypes.bfloat16)


def tile_lanes():
    count = PAIR * SEG_DEV
    order = np.zeros((TPS * LANES, count * LANES // 2))
    for t in range(TPS):
        for s in range(count):
            for c in range(HALF_PART):
                lane = s * (LANES // 2) + t * HALF_PART + c
                order[t * LANES + s * HALF_PART + c, lane] = 1.0
    return order.astype(ml_dtypes.bfloat16)


PACK_BLOCKS = 8
PACK_STEPS = NB // PACK_BLOCKS


def pack_kernel(own, records, quality, out, held, marks, order, rows, sem, mark_sem):
    lanes = PACK_BLOCKS * BLOCK

    def copy(step):
        part = records.at[:, :, pl.ds(step * lanes, lanes)]
        return pltpu.make_async_copy(part, held.at[step], sem.at[step])

    pltpu.make_async_copy(quality, marks, mark_sem).start()
    for step in range(PACK_STEPS):
        copy(step).start()
    row = lax.broadcasted_iota(jnp.int32, order.shape, 0)
    lane = lax.broadcasted_iota(jnp.int32, order.shape, 1)
    s, j = row // BLOCK, row // PART % TM
    part, at = row // HALF_PART % 2, row % HALF_PART
    target = j * BLOCK + (part * SEG_DEV + s) * HALF_PART + at
    order[...] = jnp.where(lane == target, 1.0, 0.0).astype(BF16)
    row = lax.broadcasted_iota(jnp.int32, rows.shape, 0)
    lane = lax.broadcasted_iota(jnp.int32, rows.shape, 1)
    s, n = row // ROWS, row % ROWS
    keep = (lane == n * SEG_DEV + s) & (n < SLAB)
    rows[...] = jnp.where(keep, 1.0, 0.0).astype(BF16)
    pltpu.make_async_copy(quality, marks, mark_sem).wait()
    mark = jnp.concatenate([marks[s : s + 1, :] for s in range(SEG_DEV)], axis=1)
    mark = jnp.broadcast_to(mark.astype(F32), (16, SEG_DEV * BLOCK)).astype(BF16)
    mark = jnp.dot(mark, order[...], preferred_element_type=F32)[:1]
    row = lax.broadcasted_iota(jnp.int32, (ROWS, SEG_DEV * BLOCK), 0)
    for step in range(PACK_STEPS):
        copy(step).wait()
        flat = held[step].reshape(SLAB * SEG_DEV, lanes)
        flat = jnp.dot(rows[...], flat, preferred_element_type=F32).astype(BF16)
        x = jnp.concatenate(
            [
                jnp.concatenate(
                    [
                        flat[s * ROWS : (s + 1) * ROWS, k * BLOCK : (k + 1) * BLOCK]
                        for s in range(SEG_DEV)
                    ],
                    axis=1,
                )
                for k in range(PACK_BLOCKS)
            ],
            axis=0,
        )
        y = jnp.dot(x, order[...], preferred_element_type=F32)
        for k in range(PACK_BLOCKS):
            index = step * PACK_BLOCKS + k
            extra = jnp.where((row == SLAB) & (own[0] == index), mark, 0.0)
            block = (y[k * ROWS : (k + 1) * ROWS] + extra).astype(BF16)
            for j in range(TM):
                out[index * TM + j] = block[:, j * BLOCK : (j + 1) * BLOCK]


def pack(own, records, quality):
    return pl.pallas_call(
        pack_kernel,
        out_shape=jax.ShapeDtypeStruct((NB * TM, ROWS, BLOCK), BF16),
        in_specs=[pl.BlockSpec(memory_space=pltpu.SMEM)]
        + [pl.BlockSpec(memory_space=pltpu.HBM)] * 2,
        out_specs=pl.BlockSpec(memory_space=pltpu.VMEM),
        scratch_shapes=[
            pltpu.VMEM((PACK_STEPS, SLAB, SEG_DEV, PACK_BLOCKS * BLOCK), BF16),
            pltpu.VMEM((SEG_DEV, BLOCK), jnp.int32),
            pltpu.VMEM((SEG_DEV * BLOCK, SEG_DEV * BLOCK), BF16),
            pltpu.VMEM((SEG_DEV * ROWS, SLAB * SEG_DEV), BF16),
            pltpu.SemaphoreType.DMA((PACK_STEPS,)),
            pltpu.SemaphoreType.DMA,
        ],
        compiler_params=pltpu.CompilerParams(vmem_limit_bytes=20 * MIB),
        name="pack",
    )(own, records.transpose(1, 0, 2), quality)


def whiten_kernel(own, slabs, table, inside, inverse_count, pick, low, high, sources, total):
    step = pl.program_id(0)
    lanes = []
    for i in range(PAIR):
        marks = slabs[pl.ds(own[0], 1), i, pl.ds(48, 16), :][0, SLAB - 48 : SLAB - 47, :]
        lanes.append(slabs[:, i].reshape(NB * ROWS, BLOCK) * marks)
    x = jnp.concatenate(lanes, axis=1)
    spectrum = jnp.dot(table[...], x, preferred_element_type=F32)
    re = spectrum[:F]
    im = spectrum[F:]
    magnitude = jnp.sqrt(re * re + im * im).astype(BF16)
    level = jnp.dot(inside[...], magnitude, preferred_element_type=F32) * inverse_count[...]
    inverse_level = 1.0 / (level + 1e-6)

    @pl.when(step == 0)
    def _():
        total[...] = jnp.zeros_like(total)

    first = lax.broadcasted_iota(jnp.int32, (F, LANES), 1) < LANES // 2
    for half, part in ((0, re), (1, im)):
        value = part * inverse_level
        pair = [value[:, i * BLOCK : (i + 1) * BLOCK] for i in range(PAIR)]
        turned = [pltpu.roll(one, LANES // 2, 1) for one in pair]
        low[0, half] = jnp.where(first, pair[0], turned[1]).astype(BF16)
        high[0, half] = jnp.where(first, turned[0], pair[1]).astype(BF16)
        for i in range(PAIR):
            total[...] += jnp.dot(
                pair[i].astype(BF16), pick[step * PAIR + i, half], preferred_element_type=F32
            )
    sources[...] = total[...].astype(BF16)


def whiten(own, slabs):
    inside, inverse_count = smoothing()
    shape = jax.ShapeDtypeStruct((TM // PAIR, 2, F, LANES), BF16)
    spec = pl.BlockSpec((1, 2, F, LANES), lambda i, own: (i, 0, 0, 0))
    return pl.pallas_call(
        whiten_kernel,
        out_shape=(shape, shape, jax.ShapeDtypeStruct((F, LANES), BF16)),
        grid_spec=pltpu.PrefetchScalarGridSpec(
            num_scalar_prefetch=1,
            grid=(TM // PAIR,),
            in_specs=[pl.BlockSpec((NB, PAIR, ROWS, BLOCK), lambda i, own: (0, i, 0, 0))]
            + [pl.BlockSpec(memory_space=pltpu.VMEM)] * 4,
            out_specs=(spec, spec, pl.BlockSpec((F, LANES), lambda i, own: (0, 0))),
            scratch_shapes=[pltpu.VMEM((F, LANES), F32)],
        ),
        compiler_params=pltpu.CompilerParams(vmem_limit_bytes=20 * MIB),
        name="whiten",
    )(own, slabs.reshape(NB, TM, ROWS, BLOCK), forward_table(), inside, inverse_count, source_lanes())


def choose_kernel(chan, below, above, *refs):
    outs, sem = refs[:-1], refs[-1]
    odd = lax.rem(chan[0], 2)
    count = below.shape[0] // len(outs)
    for index, out in enumerate(outs):
        for parity, ref in ((1, below), (0, above)):

            @pl.when(odd == parity)
            def _():
                part = ref.at[pl.ds(index * count, count)]
                pltpu.make_async_copy(part, out, sem.at[index]).start()

    for index, out in enumerate(outs):
        part = below.at[pl.ds(index * count, count)]
        pltpu.make_async_copy(part, out, sem.at[index]).wait()


def choose(chan, below, above, parts):
    shape = (below.shape[0] // parts, *below.shape[1:])
    return pl.pallas_call(
        choose_kernel,
        out_shape=[jax.ShapeDtypeStruct(shape, below.dtype)] * parts,
        in_specs=[pl.BlockSpec(memory_space=pltpu.SMEM)]
        + [pl.BlockSpec(memory_space=pl.ANY)] * 2,
        out_specs=[pl.BlockSpec(memory_space=pl.ANY)] * parts,
        scratch_shapes=[pltpu.SemaphoreType.DMA((parts,))],
        compiler_params=pltpu.CompilerParams(vmem_limit_bytes=MIB),
        cost_estimate=pl.CostEstimate(flops=1, bytes_accessed=1, transcendentals=0),
        name="choose",
    )(chan, below, above)


def diagonal_kernel(s0, s1, s2, s3, spread, out):
    rows = STEP
    groups = rows // GROUP
    place = pl.ds(pl.program_id(0) * groups, groups)
    row = lax.broadcasted_iota(jnp.int32, (rows, 2 * LANES), 0)
    lane = lax.broadcasted_iota(jnp.int32, (rows, 2 * LANES), 1)
    keep = jnp.bitwise_and(row, GROUP - 1) == jnp.bitwise_and(lane, GROUP - 1)
    for rel, ref in enumerate((s0, s1, s2, s3)):
        for pair in range(SRC_PART // 2):
            same, turned = [], []
            for v in (2 * pair, 2 * pair + 1):
                wide = jnp.dot(ref[...], spread[v], preferred_element_type=F32)
                wide = jnp.where(keep, wide, 0.0)
                swap = jnp.concatenate([-wide[:, LANES:], wide[:, :LANES]], axis=1)
                same.append(wide.reshape(groups, GROUP, 2 * LANES))
                turned.append(swap.reshape(groups, GROUP, 2 * LANES))
            at = (rel * SRC_PART + 2 * pair) * GROUP
            out[place, at : at + 2 * GROUP, :] = jnp.concatenate(same, axis=1).astype(BF16)
            at += SOURCES * GROUP
            out[place, at : at + 2 * GROUP, :] = jnp.concatenate(turned, axis=1).astype(BF16)


def diagonal(sources):
    wide = 2 * SOURCES * GROUP
    return pl.pallas_call(
        diagonal_kernel,
        out_shape=jax.ShapeDtypeStruct((F // GROUP, wide, 2 * LANES), BF16),
        grid=(F // STEP,),
        in_specs=[pl.BlockSpec((STEP, LANES), lambda g: (g, 0))] * TM
        + [pl.BlockSpec(memory_space=pltpu.VMEM)],
        out_specs=pl.BlockSpec(memory_space=pltpu.VMEM),
        compiler_params=pltpu.CompilerParams(vmem_limit_bytes=20 * MIB),
        cost_estimate=pl.CostEstimate(flops=1, bytes_accessed=1, transcendentals=0),
        name="diagonal",
    )(*sources, spread_lanes())


RECEIVERS = 2 * REACH + 1


def chosen(chan, tiles, t):
    offset = lax.rem(tiles[1, chan * TPS + t] - chan + REACH + NB, NB)
    mate = jnp.where(lax.rem(chan, 2) == 1, 1, 3)
    near = jnp.where(offset == REACH, 0, jnp.where(offset == mate, 3, 4))
    return jnp.where(offset == 0, 1, jnp.where(offset == 2 * REACH, 2, near))


def cross_kernel(chan, tiles, diag, order, *refs):
    receivers, (out, held, wide, sem) = refs[:-4], refs[-4:]
    step = pl.program_id(0)
    steps = F // STEP

    def copy(index, t, k):
        rows = pl.ds(k * STEP, STEP)
        refs = receivers[index:] if index == RECEIVERS - 1 else receivers[index : index + 1]
        count = held.shape[2] // len(refs)
        return [
            pltpu.make_async_copy(
                ref.at[:, :, rows, :], held.at[k, t, pl.ds(part * count, count)], sem.at[k, t]
            )
            for part, ref in enumerate(refs)
        ]

    @pl.when(step == 0)
    def _():
        picks = [chosen(chan[0], tiles, t) for t in range(TPS)]
        for k in range(steps):
            for t in range(TPS):
                for index in range(RECEIVERS):

                    @pl.when(picks[t] == index)
                    def _():
                        for one in copy(index, t, k):
                            one.start()

    for t in range(TPS):
        copy(0, t, step)[0].wait()
    x = jnp.concatenate(
        [held[step, t].reshape(TM // PAIR * 2 * STEP, LANES) for t in range(TPS)], axis=1
    )
    y = jnp.dot(x, order[...], preferred_element_type=F32)
    count = PAIR * SEG_DEV
    left = lax.broadcasted_iota(jnp.int32, (STEP, LANES), 1) < LANES // 2
    for i in range(TM // PAIR):
        for half in range(2):
            at = (i * 2 + half) * STEP
            for s in range(0, count, 2):
                one = y[at : at + STEP, s * LANES // 2 : s * LANES // 2 + LANES]
                turned = pltpu.roll(one, LANES // 2, 1)
                index = half * SEGS + i * count + s
                wide[index] = jnp.where(left, one, turned)
                wide[index + 1] = jnp.where(left, turned, one)
    first = lax.broadcasted_iota(jnp.int32, (1, GROUP, LANES), 2) < LANES // 2

    def group(pair, carry):
        outs = []
        for g in range(2):
            at = pl.multiple_of((pair * 2 + g) * GROUP, GROUP)
            b = wide[:, pl.ds(at, GROUP), :].reshape(2 * SEGS * GROUP, LANES).astype(BF16)
            o = jnp.dot(diag[step * (STEP // GROUP) + pair * 2 + g], b, preferred_element_type=F32)
            o = o.reshape(SOURCES, 2, GROUP, LANES)
            outs.append(jnp.where(first, o[:, 0], o[:, 1]))
        both = jnp.concatenate(outs, axis=1).astype(BF16)
        rows = pl.ds(pl.multiple_of(step * STEP + pair * 2 * GROUP, 2 * GROUP), 2 * GROUP)
        out[:, 0, rows, :] = both[: SOURCES // 2]
        out[:, 1, rows, :] = both[SOURCES // 2 :]
        return carry

    lax.fori_loop(0, STEP // (2 * GROUP), group, 0, unroll=UNROLL)


UNROLL = 8


def cross(chan, tiles, diag, receivers):
    return pl.pallas_call(
        cross_kernel,
        out_shape=jax.ShapeDtypeStruct((SOURCES // 2, 2, F, LANES), BF16),
        grid_spec=pltpu.PrefetchScalarGridSpec(
            num_scalar_prefetch=2,
            grid=(F // STEP,),
            in_specs=[pl.BlockSpec(memory_space=pltpu.VMEM)] * 2
            + [pl.BlockSpec(memory_space=pl.ANY)] * len(receivers),
            out_specs=pl.BlockSpec(memory_space=pltpu.VMEM),
            scratch_shapes=[
                pltpu.VMEM((F // STEP, TPS, TM // PAIR, 2, STEP, LANES), BF16),
                pltpu.VMEM((2 * SEGS, STEP, LANES), F32),
                pltpu.SemaphoreType.DMA((F // STEP, TPS)),
            ],
        ),
        compiler_params=pltpu.CompilerParams(vmem_limit_bytes=20 * MIB),
        cost_estimate=pl.CostEstimate(flops=1, bytes_accessed=1, transcendentals=0),
        name="cross",
    )(chan, tiles, diag, tile_lanes(), *receivers)


def stack_kernel(rel, spectra, inverse, out):
    first = rel * SRC_PART // 2
    x = jnp.concatenate(
        [spectra[first + pair].reshape(2 * F, LANES) for pair in range(SRC_PART // 2)], axis=1
    )
    y = jnp.dot(inverse[...], x, preferred_element_type=F32)
    for pair in range(SRC_PART // 2):
        value = y[:, pair * LANES : (pair + 1) * LANES].T.astype(BF16)
        for v in range(2):
            for t in range(TPS):
                at = (t * SRC_PART + 2 * pair + v) * HALF_PART
                row = v * (LANES // 2) + t * HALF_PART
                out[at : at + HALF_PART, :] = value[row : row + HALF_PART, :]


def stack(spectra, rel, inverse):
    rows = TPS * SRC_PART * HALF_PART
    return pl.pallas_call(
        functools.partial(stack_kernel, rel),
        out_shape=jax.ShapeDtypeStruct((rows, LAG_COUNT), BF16),
        in_specs=[pl.BlockSpec(memory_space=pltpu.VMEM)] * 2,
        out_specs=pl.BlockSpec(memory_space=pltpu.VMEM),
        compiler_params=pltpu.CompilerParams(vmem_limit_bytes=10 * MIB),
        cost_estimate=pl.CostEstimate(flops=1, bytes_accessed=1, transcendentals=0),
        name="stack",
    )(spectra, inverse)


def merge_kernel(*refs):
    pieces, out, sem = refs[:TM], refs[TM], refs[TM + 1]
    rows = pieces[0].shape[0]
    copies = [
        pltpu.make_async_copy(ref, out.at[pl.ds(rel * rows, rows), :], sem.at[rel])
        for rel, ref in enumerate(pieces)
    ]
    for copy in copies:
        copy.start()
    for copy in copies:
        copy.wait()


def merge(pieces):
    rows, width = pieces[0].shape
    return pl.pallas_call(
        merge_kernel,
        out_shape=jax.ShapeDtypeStruct((TM * rows, width), pieces[0].dtype),
        in_specs=[pl.BlockSpec(memory_space=pl.ANY)] * TM,
        out_specs=pl.BlockSpec(memory_space=pl.ANY),
        scratch_shapes=[pltpu.SemaphoreType.DMA((TM,))],
        compiler_params=pltpu.CompilerParams(vmem_limit_bytes=MIB),
        cost_estimate=pl.CostEstimate(flops=1, bytes_accessed=1, transcendentals=0),
        name="merge",
    )(*pieces)


def arrange(time, pieces, t):
    rows = SRC_PART * HALF_PART
    parts = []
    for ref in pieces:
        count = ref.shape[0] // (TPS * rows)
        parts += [(ref, part * TPS * rows) for part in range(count)]
    for index, (ref, first) in enumerate(parts):
        half, rel = divmod(index, TM)
        value = ref[first + t * rows : first + (t + 1) * rows, :].astype(F32)
        at = lax.rem(time + TM - rel, TM) * PART + half * HALF_PART
        yield pl.multiple_of(at, HALF_PART), value.reshape(SRC_PART, HALF_PART, LAG_COUNT)


def home_kernel(owners, chan, time, *refs):
    pieces, out = refs[:-1], refs[-1]
    slot = pl.program_id(0)
    out[...] = jnp.zeros_like(out)
    for t in range(TPS):

        @pl.when(owners[chan[0] * TPS + t] == chan[0] * TCAP + slot)
        def _():
            for at, value in arrange(time[0], pieces, t):
                out[0, :, pl.ds(at, HALF_PART), :] = value


def home(owners, chan, time, pieces):
    return pl.pallas_call(
        home_kernel,
        out_shape=jax.ShapeDtypeStruct((TCAP, SRC_PART, BLOCK, LAG_COUNT), F32),
        grid_spec=pltpu.PrefetchScalarGridSpec(
            num_scalar_prefetch=3,
            grid=(TCAP,),
            in_specs=[pl.BlockSpec(memory_space=pltpu.VMEM) for _ in pieces],
            out_specs=pl.BlockSpec((1, SRC_PART, BLOCK, LAG_COUNT), lambda s, *_: (s, 0, 0, 0)),
        ),
        compiler_params=pltpu.CompilerParams(vmem_limit_bytes=10 * MIB),
        cost_estimate=pl.CostEstimate(flops=1, bytes_accessed=1, transcendentals=0),
        name="home",
    )(owners, chan, time, *pieces)


def moved_kernel(owners, chan, time, *refs):
    pieces, (_, out, held, sem) = refs[:-4], refs[-4:]
    source = lax.rem(chan[0] + NB - 1, NB)
    copies = []
    for t in range(TPS):
        slot = owners[source * TPS + t] - chan[0] * TCAP
        mine = (slot >= 0) & (slot < TCAP)
        copy = pltpu.make_async_copy(held.at[t], out.at[jnp.clip(slot, 0, TCAP - 1)], sem.at[t])
        copies.append((mine, copy))

        @pl.when(mine)
        def _():
            for at, value in arrange(time[0], pieces, t):
                held[t, :, pl.ds(at, HALF_PART), :] = value
            copy.start()

    for mine, copy in copies:

        @pl.when(mine)
        def _():
            copy.wait()


def moved(owners, chan, time, pieces, result):
    return pl.pallas_call(
        moved_kernel,
        out_shape=jax.ShapeDtypeStruct(result.shape, result.dtype),
        in_specs=[pl.BlockSpec(memory_space=pltpu.SMEM)] * 3
        + [pl.BlockSpec(memory_space=pltpu.VMEM) for _ in pieces]
        + [pl.BlockSpec(memory_space=pl.ANY)],
        out_specs=pl.BlockSpec(memory_space=pl.ANY),
        scratch_shapes=[
            pltpu.VMEM((TPS, SRC_PART, BLOCK, LAG_COUNT), F32),
            pltpu.SemaphoreType.DMA((TPS,)),
        ],
        input_output_aliases={3 + len(pieces): 0},
        compiler_params=pltpu.CompilerParams(vmem_limit_bytes=12 * MIB),
        cost_estimate=pl.CostEstimate(flops=1, bytes_accessed=1, transcendentals=0),
        name="moved",
    )(owners, chan, time, *pieces, result)


def shifted(value, axis, distance):
    count = lax.axis_size(axis)
    return lax.ppermute(value, axis, [(i, (i + distance) % count) for i in range(count)])


def per_device(records, quality, tile_list, tile_slot_owner):
    chan = lax.axis_index("chan").astype(jnp.int32).reshape(1)
    time = lax.axis_index("tm").astype(jnp.int32).reshape(1)
    tiles = tile_list.T
    swap = [(i, i ^ 1) for i in range(NB)]

    slabs = pack(chan, records, quality)
    slabs = lax.all_to_all(slabs, ("chan", "tm"), split_axis=0, concat_axis=0, tiled=True)
    low, high, sources = whiten(chan, slabs)
    sources = [sources] + [shifted(sources, "tm", -rel) for rel in range(1, TM)]

    def halo(white):
        mate = lax.ppermute(white, "chan", swap)
        return [white, shifted(white, "chan", 2), shifted(white, "chan", -2), mate]

    def complete(blocks, parts):
        others = choose(chan, blocks[1], blocks[2], parts)
        return blocks + [lax.ppermute(other, "chan", swap) for other in others]

    inverse = inverse_table()
    order = (2, 0, 1, 3)
    low = halo(low)
    high, low[3] = lax.optimization_barrier((high, low[3]))
    high = halo(high)
    low, sources = lax.optimization_barrier((low, sources))
    diag = diagonal(sources)
    spectra = cross(chan, tiles, diag, complete(low, 2))
    parts = [stack(spectra, rel, inverse) for rel in range(TM)]
    stay_low = [shifted(part, "tm", rel) if rel else part for rel, part in enumerate(parts)]
    high, _ = lax.optimization_barrier((high, parts))
    high = complete(high, 1)
    spectra = cross(chan, tiles, diag, high)
    spectra, stay_low = lax.optimization_barrier((spectra, stay_low))
    move_low = shifted(merge(stay_low), "chan", 1)
    stay_high, move_high = [None] * TM, [None] * TM
    for rel in order:
        part = stack(spectra, rel, inverse)
        stay_high[rel] = shifted(part, "tm", rel) if rel else part
        if rel == 3:
            stay_high[rel], move_low = lax.optimization_barrier((stay_high[rel], move_low))
        move_high[rel] = shifted(stay_high[rel], "chan", 1)
    result = home(tile_slot_owner, chan, time, stay_low + stay_high)
    return moved(tile_slot_owner, chan, time, [move_low] + move_high, result)


def solution(mesh):
    placed = (P("tm", "chan", None), P("tm", "chan"), P(), P())
    return jax.shard_map(
        per_device,
        mesh=mesh,
        in_specs=placed,
        out_specs=P("chan", "tm", None, None),
        check_vma=False,
    )
```

```python
import functools
import math

import jax
import jax.numpy as jnp
import ml_dtypes
import numpy as np
from jax import lax
from jax.experimental import pallas as pl
from jax.experimental.pallas import tpu as pltpu
from jax.sharding import PartitionSpec as P

L = 1920
F = 768
K0 = 8
HALF = 32
LAG_COUNT = 512
BLOCK = 128
SOURCES = 16
TPS = 3
REACH = 2
SEG_DEV = 4
SEGS = 16
NB = 32
TCAP = 6
TM = 4
SLAB = L // NB
ROWS = 64
PART = BLOCK // TM
SRC_PART = SOURCES // TM
MIB = 1 << 20
LANES = 128
GROUP = 8
STEP = 128
HALF_PART = PART // 2

BF16 = jnp.bfloat16
F32 = jnp.float32


def forward_table():
    n = np.arange(L)[None, :]
    q = K0 + np.arange(F)[:, None]
    angles = (n * q % L) * (2.0 * np.pi / L)
    window = 0.5 - 0.5 * np.cos(np.arange(L) * (2.0 * np.pi / L))
    table = np.concatenate([np.cos(angles), -np.sin(angles)], axis=0) * window[None, :]
    padded = np.zeros((2 * F, NB, ROWS))
    padded[:, :, :SLAB] = table.reshape(2 * F, NB, SLAB)
    return padded.reshape(2 * F, NB * ROWS).astype(ml_dtypes.bfloat16)


def smoothing():
    k = np.arange(F)
    inside = (np.abs(k[:, None] - k[None, :]) <= HALF).astype(np.float64)
    inverse_count = 1.0 / inside.sum(axis=1, keepdims=True)
    return inside.astype(ml_dtypes.bfloat16), inverse_count.astype(np.float32)


def inverse_table():
    q = K0 + np.arange(F)[None, :]
    lag = np.arange(LAG_COUNT)[:, None] - LAG_COUNT // 2
    angles = (q * lag % L) * (2.0 * np.pi / L)
    table = np.concatenate([np.cos(angles), -np.sin(angles)], axis=1) / math.sqrt(SEGS * F)
    return table.astype(ml_dtypes.bfloat16)


PAIR = 2
PARTS = TM // PAIR


def source_lanes():
    pick = np.zeros((TM, 2, BLOCK, LANES))
    for i in range(TM):
        for half in range(2):
            for s in range(SEG_DEV):
                for v in range(SRC_PART):
                    part, at = divmod(v * (BLOCK // SOURCES), HALF_PART)
                    lane = half * SRC_PART * SEGS + v * SEGS + i * SEG_DEV + s
                    pick[i, half, (part * SEG_DEV + s) * HALF_PART + at, lane] = 1.0
    return pick.astype(ml_dtypes.bfloat16)


def spread_lanes():
    spread = np.zeros((SRC_PART, LANES, 2 * LANES))
    for v in range(SRC_PART):
        for half in range(2):
            for s in range(SEGS):
                lane = half * LANES + s * GROUP
                spread[v, half * SRC_PART * SEGS + v * SEGS + s, lane : lane + GROUP] = 1.0
    return spread.astype(ml_dtypes.bfloat16)


def tile_lanes():
    count = PAIR * SEG_DEV
    order = np.zeros((TPS * LANES, count * LANES // 2))
    for t in range(TPS):
        for s in range(count):
            for c in range(HALF_PART):
                lane = s * (LANES // 2) + t * HALF_PART + c
                order[t * LANES + s * HALF_PART + c, lane] = 1.0
    return order.astype(ml_dtypes.bfloat16)


PACK_BLOCKS = 8
PACK_STEPS = NB // PACK_BLOCKS


def pack_kernel(own, records, quality, out, held, marks, order, rows, sem, mark_sem):
    lanes = PACK_BLOCKS * BLOCK

    def copy(step):
        part = records.at[:, :, pl.ds(step * lanes, lanes)]
        return pltpu.make_async_copy(part, held.at[step], sem.at[step])

    pltpu.make_async_copy(quality, marks, mark_sem).start()
    for step in range(PACK_STEPS):
        copy(step).start()
    row = lax.broadcasted_iota(jnp.int32, order.shape, 0)
    lane = lax.broadcasted_iota(jnp.int32, order.shape, 1)
    s, j = row // BLOCK, row // PART % TM
    part, at = row // HALF_PART % 2, row % HALF_PART
    target = j * BLOCK + (part * SEG_DEV + s) * HALF_PART + at
    order[...] = jnp.where(lane == target, 1.0, 0.0).astype(BF16)
    row = lax.broadcasted_iota(jnp.int32, rows.shape, 0)
    lane = lax.broadcasted_iota(jnp.int32, rows.shape, 1)
    s, n = row // ROWS, row % ROWS
    keep = (lane == n * SEG_DEV + s) & (n < SLAB)
    rows[...] = jnp.where(keep, 1.0, 0.0).astype(BF16)
    pltpu.make_async_copy(quality, marks, mark_sem).wait()
    mark = jnp.concatenate([marks[s : s + 1, :] for s in range(SEG_DEV)], axis=1)
    mark = jnp.broadcast_to(mark.astype(F32), (16, SEG_DEV * BLOCK)).astype(BF16)
    mark = jnp.dot(mark, order[...], preferred_element_type=F32)[:1]
    row = lax.broadcasted_iota(jnp.int32, (ROWS, SEG_DEV * BLOCK), 0)
    for step in range(PACK_STEPS):
        copy(step).wait()
        flat = held[step].reshape(SLAB * SEG_DEV, lanes)
        flat = jnp.dot(rows[...], flat, preferred_element_type=F32).astype(BF16)
        x = jnp.concatenate(
            [
                jnp.concatenate(
                    [
                        flat[s * ROWS : (s + 1) * ROWS, k * BLOCK : (k + 1) * BLOCK]
                        for s in range(SEG_DEV)
                    ],
                    axis=1,
                )
                for k in range(PACK_BLOCKS)
            ],
            axis=0,
        )
        y = jnp.dot(x, order[...], preferred_element_type=F32)
        for k in range(PACK_BLOCKS):
            index = step * PACK_BLOCKS + k
            extra = jnp.where((row == SLAB) & (own[0] == index), mark, 0.0)
            block = (y[k * ROWS : (k + 1) * ROWS] + extra).astype(BF16)
            for j in range(TM):
                out[index * TM + j] = block[:, j * BLOCK : (j + 1) * BLOCK]


def pack(own, records, quality):
    return pl.pallas_call(
        pack_kernel,
        out_shape=jax.ShapeDtypeStruct((NB * TM, ROWS, BLOCK), BF16),
        in_specs=[pl.BlockSpec(memory_space=pltpu.SMEM)]
        + [pl.BlockSpec(memory_space=pltpu.HBM)] * 2,
        out_specs=pl.BlockSpec(memory_space=pltpu.VMEM),
        scratch_shapes=[
            pltpu.VMEM((PACK_STEPS, SLAB, SEG_DEV, PACK_BLOCKS * BLOCK), BF16),
            pltpu.VMEM((SEG_DEV, BLOCK), jnp.int32),
            pltpu.VMEM((SEG_DEV * BLOCK, SEG_DEV * BLOCK), BF16),
            pltpu.VMEM((SEG_DEV * ROWS, SLAB * SEG_DEV), BF16),
            pltpu.SemaphoreType.DMA((PACK_STEPS,)),
            pltpu.SemaphoreType.DMA,
        ],
        compiler_params=pltpu.CompilerParams(vmem_limit_bytes=20 * MIB),
        name="pack",
    )(own, records.transpose(1, 0, 2), quality)


def whiten_kernel(own, slabs, table, inside, inverse_count, pick, low, high, sources):
    first = lax.broadcasted_iota(jnp.int32, (F, LANES), 1) < LANES // 2
    total = jnp.zeros((F, LANES), F32)
    spectra = []
    for step in range(PARTS):
        lanes = []
        for i in range(PAIR):
            at = step * PAIR + i
            marks = slabs[pl.ds(own[0], 1), at, pl.ds(48, 16), :][0, SLAB - 48 : SLAB - 47, :]
            lanes.append(slabs[:, at].reshape(NB * ROWS, BLOCK) * marks)
        x = jnp.concatenate(lanes, axis=1)
        spectra.append(jnp.dot(table[...], x, preferred_element_type=F32))
    for step, spectrum in enumerate(spectra):
        re = spectrum[:F]
        im = spectrum[F:]
        magnitude = jnp.sqrt(re * re + im * im).astype(BF16)
        level = jnp.dot(inside[...], magnitude, preferred_element_type=F32) * inverse_count[...]
        inverse_level = 1.0 / (level + 1e-6)
        for half, part in ((0, re), (1, im)):
            value = part * inverse_level
            pair = [value[:, i * BLOCK : (i + 1) * BLOCK] for i in range(PAIR)]
            turned = [pltpu.roll(one, LANES // 2, 1) for one in pair]
            low[step, half] = jnp.where(first, pair[0], turned[1]).astype(BF16)
            high[step, half] = jnp.where(first, turned[0], pair[1]).astype(BF16)
            for i in range(PAIR):
                total += jnp.dot(
                    pair[i].astype(BF16), pick[step * PAIR + i, half], preferred_element_type=F32
                )
    sources[...] = total.astype(BF16)


def whiten(own, slabs):
    inside, inverse_count = smoothing()
    shape = jax.ShapeDtypeStruct((PARTS, 2, F, LANES), BF16)
    return pl.pallas_call(
        whiten_kernel,
        out_shape=(shape, shape, jax.ShapeDtypeStruct((F, LANES), BF16)),
        in_specs=[pl.BlockSpec(memory_space=pltpu.SMEM)]
        + [pl.BlockSpec(memory_space=pltpu.VMEM)] * 5,
        out_specs=[pl.BlockSpec(memory_space=pltpu.VMEM)] * 3,
        compiler_params=pltpu.CompilerParams(vmem_limit_bytes=24 * MIB),
        name="whiten",
    )(own, slabs.reshape(NB, TM, ROWS, BLOCK), forward_table(), inside, inverse_count, source_lanes())


def choose_kernel(chan, below, above, *refs):
    outs, sem = refs[:-1], refs[-1]
    odd = lax.rem(chan[0], 2)
    count = below.shape[0] // len(outs)
    for index, out in enumerate(outs):
        for parity, ref in ((1, below), (0, above)):

            @pl.when(odd == parity)
            def _():
                part = ref.at[pl.ds(index * count, count)]
                pltpu.make_async_copy(part, out, sem.at[index]).start()

    for index, out in enumerate(outs):
        part = below.at[pl.ds(index * count, count)]
        pltpu.make_async_copy(part, out, sem.at[index]).wait()


def choose(chan, below, above, parts):
    shape = (below.shape[0] // parts, *below.shape[1:])
    return pl.pallas_call(
        choose_kernel,
        out_shape=[jax.ShapeDtypeStruct(shape, below.dtype)] * parts,
        in_specs=[pl.BlockSpec(memory_space=pltpu.SMEM)]
        + [pl.BlockSpec(memory_space=pl.ANY)] * 2,
        out_specs=[pl.BlockSpec(memory_space=pl.ANY)] * parts,
        scratch_shapes=[pltpu.SemaphoreType.DMA((parts,))],
        compiler_params=pltpu.CompilerParams(vmem_limit_bytes=MIB),
        cost_estimate=pl.CostEstimate(flops=1, bytes_accessed=1, transcendentals=0),
        name="choose",
    )(chan, below, above)


def diagonal_kernel(s0, s1, s2, s3, spread, out):
    row = lax.broadcasted_iota(jnp.int32, (F, 2 * LANES), 0)
    lane = lax.broadcasted_iota(jnp.int32, (F, 2 * LANES), 1)
    keep = jnp.bitwise_and(row, GROUP - 1) == jnp.bitwise_and(lane, GROUP - 1)
    for rel, ref in enumerate((s0, s1, s2, s3)):
        for pair in range(SRC_PART // 2):
            wides = []
            for v in (2 * pair, 2 * pair + 1):
                wide = jnp.dot(ref[...], spread[v], preferred_element_type=F32)
                wide = jnp.where(keep, wide, 0.0)
                wides.append(wide.reshape(F // GROUP, GROUP, 2 * LANES))
            at = (rel * SRC_PART + 2 * pair) * GROUP
            out[:, at : at + 2 * GROUP, :] = jnp.concatenate(wides, axis=1).astype(BF16)


def diagonal(sources):
    return pl.pallas_call(
        diagonal_kernel,
        out_shape=jax.ShapeDtypeStruct((F // GROUP, SOURCES * GROUP, 2 * LANES), BF16),
        in_specs=[pl.BlockSpec(memory_space=pltpu.VMEM)] * (TM + 1),
        out_specs=pl.BlockSpec(memory_space=pltpu.VMEM),
        compiler_params=pltpu.CompilerParams(vmem_limit_bytes=20 * MIB),
        cost_estimate=pl.CostEstimate(flops=1, bytes_accessed=1, transcendentals=0),
        name="diagonal",
    )(*sources, spread_lanes())


RECEIVERS = 2 * REACH + 1


def chosen(chan, tiles, t):
    offset = lax.rem(tiles[1, chan * TPS + t] - chan + REACH + NB, NB)
    mate = jnp.where(lax.rem(chan, 2) == 1, 1, 3)
    near = jnp.where(offset == REACH, 0, jnp.where(offset == mate, 3, 4))
    return jnp.where(offset == 0, 1, jnp.where(offset == 2 * REACH, 2, near))


def cross_kernel(chan, tiles, diag, order, *refs):
    receivers, (out, held, wide, sem) = refs[:-4], refs[-4:]
    step = pl.program_id(0)
    steps = F // STEP

    def copy(index, t, k):
        rows = pl.ds(k * STEP, STEP)
        refs = receivers[index:] if index == RECEIVERS - 1 else receivers[index : index + 1]
        count = held.shape[2] // len(refs)
        return [
            pltpu.make_async_copy(
                ref.at[:, :, rows, :], held.at[k, t, pl.ds(part * count, count)], sem.at[k, t]
            )
            for part, ref in enumerate(refs)
        ]

    @pl.when(step == 0)
    def _():
        picks = [chosen(chan[0], tiles, t) for t in range(TPS)]
        for k in range(steps):
            for t in range(TPS):
                for index in range(RECEIVERS):

                    @pl.when(picks[t] == index)
                    def _():
                        for one in copy(index, t, k):
                            one.start()

    for t in range(TPS):
        copy(0, t, step)[0].wait()
    x = jnp.concatenate(
        [held[step, t].reshape(TM // PAIR * 2 * STEP, LANES) for t in range(TPS)], axis=1
    )
    y = jnp.dot(x, order[...], preferred_element_type=F32)
    count = PAIR * SEG_DEV
    left = lax.broadcasted_iota(jnp.int32, (STEP, LANES), 1) < LANES // 2
    for i in range(TM // PAIR):
        at = i * 2 * STEP
        for s in range(0, count, 2):
            lanes = slice(s * LANES // 2, s * LANES // 2 + LANES)
            re = y[at : at + STEP, lanes]
            im = y[at + STEP : at + 2 * STEP, lanes]
            re_turned = pltpu.roll(re, LANES // 2, 1)
            im_turned = pltpu.roll(im, LANES // 2, 1)
            index = i * count + s
            wide[index] = jnp.where(left, re, im_turned)
            wide[index + 1] = jnp.where(left, re_turned, im)
            wide[SEGS + index] = jnp.where(left, im, -re_turned)
            wide[SEGS + index + 1] = jnp.where(left, im_turned, -re)
    first = lax.broadcasted_iota(jnp.int32, (1, GROUP, LANES), 2) < LANES // 2

    def group(pair, carry):
        parts = [], []
        for g in range(2):
            at = pl.multiple_of((pair * 2 + g) * GROUP, GROUP)
            b = wide[:, pl.ds(at, GROUP), :].reshape(2 * SEGS * GROUP, LANES).astype(BF16)
            o = jnp.dot(
                diag[step * (STEP // GROUP) + pair * 2 + g], b, preferred_element_type=F32
            )
            turned = pltpu.roll(o, LANES // 2, 1).reshape(SOURCES // 2, 2, GROUP, LANES)
            o = o.reshape(SOURCES // 2, 2, GROUP, LANES)
            parts[0].append(jnp.where(first, o[:, 0], turned[:, 1]))
            parts[1].append(jnp.where(first, turned[:, 0], o[:, 1]))
        rows = pl.ds(pl.multiple_of(step * STEP + pair * 2 * GROUP, 2 * GROUP), 2 * GROUP)
        for half in range(2):
            out[:, half, rows, :] = jnp.concatenate(parts[half], axis=1).astype(BF16)
        return carry

    lax.fori_loop(0, STEP // (2 * GROUP), group, 0, unroll=UNROLL)


UNROLL = 8


def cross(chan, tiles, diag, receivers):
    return pl.pallas_call(
        cross_kernel,
        out_shape=jax.ShapeDtypeStruct((SOURCES // 2, 2, F, LANES), BF16),
        grid_spec=pltpu.PrefetchScalarGridSpec(
            num_scalar_prefetch=2,
            grid=(F // STEP,),
            in_specs=[pl.BlockSpec(memory_space=pltpu.VMEM)] * 2
            + [pl.BlockSpec(memory_space=pl.ANY)] * len(receivers),
            out_specs=pl.BlockSpec(memory_space=pltpu.VMEM),
            scratch_shapes=[
                pltpu.VMEM((F // STEP, TPS, TM // PAIR, 2, STEP, LANES), BF16),
                pltpu.VMEM((2 * SEGS, STEP, LANES), F32),
                pltpu.SemaphoreType.DMA((F // STEP, TPS)),
            ],
        ),
        compiler_params=pltpu.CompilerParams(vmem_limit_bytes=20 * MIB),
        cost_estimate=pl.CostEstimate(flops=1, bytes_accessed=1, transcendentals=0),
        name="cross",
    )(chan, tiles, diag, tile_lanes(), *receivers)


def stack_kernel(rels, spectra, inverse, *outs):
    for rel, out in zip(rels, outs):
        first = rel * SRC_PART // 2
        x = jnp.concatenate(
            [spectra[first + pair].reshape(2 * F, LANES) for pair in range(SRC_PART // 2)], axis=1
        )
        y = jnp.dot(inverse[...], x, preferred_element_type=F32)
        for pair in range(SRC_PART // 2):
            value = y[:, pair * LANES : (pair + 1) * LANES].T.astype(BF16)
            for v in range(2):
                for t in range(TPS):
                    at = (t * SRC_PART + 2 * pair + v) * HALF_PART
                    row = v * (LANES // 2) + t * HALF_PART
                    out[at : at + HALF_PART, :] = value[row : row + HALF_PART, :]


def stack(spectra, rels, inverse):
    rows = TPS * SRC_PART * HALF_PART
    return pl.pallas_call(
        functools.partial(stack_kernel, rels),
        out_shape=[jax.ShapeDtypeStruct((rows, LAG_COUNT), BF16)] * len(rels),
        in_specs=[pl.BlockSpec(memory_space=pltpu.VMEM)] * 2,
        out_specs=[pl.BlockSpec(memory_space=pltpu.VMEM)] * len(rels),
        compiler_params=pltpu.CompilerParams(vmem_limit_bytes=12 * MIB),
        cost_estimate=pl.CostEstimate(flops=1, bytes_accessed=1, transcendentals=0),
        name="stack",
    )(spectra, inverse)


def merge_kernel(*refs):
    pieces, out, sem = refs[:TM], refs[TM], refs[TM + 1]
    rows = pieces[0].shape[0]
    copies = [
        pltpu.make_async_copy(ref, out.at[pl.ds(rel * rows, rows), :], sem.at[rel])
        for rel, ref in enumerate(pieces)
    ]
    for copy in copies:
        copy.start()
    for copy in copies:
        copy.wait()


def merge(pieces):
    rows, width = pieces[0].shape
    return pl.pallas_call(
        merge_kernel,
        out_shape=jax.ShapeDtypeStruct((TM * rows, width), pieces[0].dtype),
        in_specs=[pl.BlockSpec(memory_space=pl.ANY)] * TM,
        out_specs=pl.BlockSpec(memory_space=pl.ANY),
        scratch_shapes=[pltpu.SemaphoreType.DMA((TM,))],
        compiler_params=pltpu.CompilerParams(vmem_limit_bytes=MIB),
        cost_estimate=pl.CostEstimate(flops=1, bytes_accessed=1, transcendentals=0),
        name="merge",
    )(*pieces)


def arrange(time, pieces, t):
    rows = SRC_PART * HALF_PART
    parts = []
    for ref in pieces:
        count = ref.shape[0] // (TPS * rows)
        parts += [(ref, part * TPS * rows) for part in range(count)]
    for index, (ref, first) in enumerate(parts):
        half, rel = divmod(index, TM)
        value = ref[first + t * rows : first + (t + 1) * rows, :].astype(F32)
        at = lax.rem(time + TM - rel, TM) * PART + half * HALF_PART
        yield pl.multiple_of(at, HALF_PART), value.reshape(SRC_PART, HALF_PART, LAG_COUNT)


def home_kernel(owners, chan, time, *refs):
    pieces, out = refs[:-1], refs[-1]
    slot = pl.program_id(0)
    out[...] = jnp.zeros_like(out)
    for t in range(TPS):

        @pl.when(owners[chan[0] * TPS + t] == chan[0] * TCAP + slot)
        def _():
            for at, value in arrange(time[0], pieces, t):
                out[0, :, pl.ds(at, HALF_PART), :] = value


def home(owners, chan, time, pieces):
    return pl.pallas_call(
        home_kernel,
        out_shape=jax.ShapeDtypeStruct((TCAP, SRC_PART, BLOCK, LAG_COUNT), F32),
        grid_spec=pltpu.PrefetchScalarGridSpec(
            num_scalar_prefetch=3,
            grid=(TCAP,),
            in_specs=[pl.BlockSpec(memory_space=pltpu.VMEM) for _ in pieces],
            out_specs=pl.BlockSpec((1, SRC_PART, BLOCK, LAG_COUNT), lambda s, *_: (s, 0, 0, 0)),
        ),
        compiler_params=pltpu.CompilerParams(vmem_limit_bytes=10 * MIB),
        cost_estimate=pl.CostEstimate(flops=1, bytes_accessed=1, transcendentals=0),
        name="home",
    )(owners, chan, time, *pieces)


def moved_kernel(owners, chan, time, *refs):
    pieces, (_, out, held, sem) = refs[:-4], refs[-4:]
    source = lax.rem(chan[0] + NB - 1, NB)
    copies = []
    for t in range(TPS):
        slot = owners[source * TPS + t] - chan[0] * TCAP
        mine = (slot >= 0) & (slot < TCAP)
        copy = pltpu.make_async_copy(held.at[t], out.at[jnp.clip(slot, 0, TCAP - 1)], sem.at[t])
        copies.append((mine, copy))

        @pl.when(mine)
        def _():
            for at, value in arrange(time[0], pieces, t):
                held[t, :, pl.ds(at, HALF_PART), :] = value
            copy.start()

    for mine, copy in copies:

        @pl.when(mine)
        def _():
            copy.wait()


def moved(owners, chan, time, pieces, result):
    return pl.pallas_call(
        moved_kernel,
        out_shape=jax.ShapeDtypeStruct(result.shape, result.dtype),
        in_specs=[pl.BlockSpec(memory_space=pltpu.SMEM)] * 3
        + [pl.BlockSpec(memory_space=pltpu.VMEM) for _ in pieces]
        + [pl.BlockSpec(memory_space=pl.ANY)],
        out_specs=pl.BlockSpec(memory_space=pl.ANY),
        scratch_shapes=[
            pltpu.VMEM((TPS, SRC_PART, BLOCK, LAG_COUNT), F32),
            pltpu.SemaphoreType.DMA((TPS,)),
        ],
        input_output_aliases={3 + len(pieces): 0},
        compiler_params=pltpu.CompilerParams(vmem_limit_bytes=12 * MIB),
        cost_estimate=pl.CostEstimate(flops=1, bytes_accessed=1, transcendentals=0),
        name="moved",
    )(owners, chan, time, *pieces, result)


def shifted(value, axis, distance):
    count = lax.axis_size(axis)
    return lax.ppermute(value, axis, [(i, (i + distance) % count) for i in range(count)])


def per_device(records, quality, tile_list, tile_slot_owner):
    chan = lax.axis_index("chan").astype(jnp.int32).reshape(1)
    time = lax.axis_index("tm").astype(jnp.int32).reshape(1)
    tiles = tile_list.T
    swap = [(i, i ^ 1) for i in range(NB)]

    slabs = pack(chan, records, quality)
    slabs = lax.all_to_all(slabs, ("chan", "tm"), split_axis=0, concat_axis=0, tiled=True)
    low, high, sources = whiten(chan, slabs)
    sources = [sources] + [shifted(sources, "tm", -rel) for rel in range(1, TM)]

    def halo(white):
        mate = lax.ppermute(white, "chan", swap)
        return [white, shifted(white, "chan", 2), shifted(white, "chan", -2), mate]

    def complete(blocks, parts):
        others = choose(chan, blocks[1], blocks[2], parts)
        return blocks + [lax.ppermute(other, "chan", swap) for other in others]

    inverse = inverse_table()
    order = (2, 0, 1, 3)
    low = halo(low)
    high, low[3] = lax.optimization_barrier((high, low[3]))
    high = halo(high)
    low, sources = lax.optimization_barrier((low, sources))
    diag = diagonal(sources)
    spectra = cross(chan, tiles, diag, complete(low, 2))
    parts = stack(spectra, tuple(range(TM)), inverse)
    stay_low = [shifted(part, "tm", rel) if rel else part for rel, part in enumerate(parts)]
    high, _ = lax.optimization_barrier((high, parts))
    high = complete(high, 1)
    spectra = cross(chan, tiles, diag, high)
    spectra, stay_low = lax.optimization_barrier((spectra, stay_low))
    move_low = shifted(merge(stay_low), "chan", 1)
    stay_high, move_high = [None] * TM, [None] * TM
    for rel in order:
        (part,) = stack(spectra, (rel,), inverse)
        stay_high[rel] = shifted(part, "tm", rel) if rel else part
        if rel == 2:
            stay_high[rel], move_low = lax.optimization_barrier((stay_high[rel], move_low))
        move_high[rel] = shifted(stay_high[rel], "chan", 1)
    result = home(tile_slot_owner, chan, time, stay_low + stay_high)
    return moved(tile_slot_owner, chan, time, [move_low] + move_high, result)


def solution(mesh):
    placed = (P("tm", "chan", None), P("tm", "chan"), P(), P())
    return jax.shard_map(
        per_device,
        mesh=mesh,
        in_specs=placed,
        out_specs=P("chan", "tm", None, None),
        check_vma=False,
    )
```

```python
import functools
import math

import jax
import jax.numpy as jnp
import ml_dtypes
import numpy as np
from jax import lax
from jax.experimental import pallas as pl
from jax.experimental.pallas import tpu as pltpu
from jax.sharding import PartitionSpec as P

L = 1920
F = 768
K0 = 8
HALF = 32
LAG_COUNT = 512
BLOCK = 128
SOURCES = 16
TPS = 3
REACH = 2
SEG_DEV = 4
SEGS = 16
NB = 32
TCAP = 6
TM = 4
SLAB = L // NB
ROWS = 64
PART = BLOCK // TM
SRC_PART = SOURCES // TM
MIB = 1 << 20
LANES = 128
GROUP = 8
STEP = 128
HALF_PART = PART // 2

BF16 = jnp.bfloat16
F32 = jnp.float32


def forward_table():
    n = np.arange(L)[None, :]
    q = K0 + np.arange(F)[:, None]
    angles = (n * q % L) * (2.0 * np.pi / L)
    window = 0.5 - 0.5 * np.cos(np.arange(L) * (2.0 * np.pi / L))
    table = np.concatenate([np.cos(angles), -np.sin(angles)], axis=0) * window[None, :]
    padded = np.zeros((2 * F, NB, ROWS))
    padded[:, :, :SLAB] = table.reshape(2 * F, NB, SLAB)
    return padded.reshape(2 * F, NB * ROWS).astype(ml_dtypes.bfloat16)


def smoothing():
    k = np.arange(F)
    inside = (np.abs(k[:, None] - k[None, :]) <= HALF).astype(np.float64)
    inverse_count = 1.0 / inside.sum(axis=1, keepdims=True)
    return inside.astype(ml_dtypes.bfloat16), inverse_count.astype(np.float32)


def inverse_table():
    q = K0 + np.arange(F)[None, :]
    lag = np.arange(LAG_COUNT)[:, None] - LAG_COUNT // 2
    angles = (q * lag % L) * (2.0 * np.pi / L)
    table = np.concatenate([np.cos(angles), -np.sin(angles)], axis=1) / math.sqrt(SEGS * F)
    return table.astype(ml_dtypes.bfloat16)


PAIR = 2
PARTS = TM // PAIR


def source_lanes():
    pick = np.zeros((PARTS, 2, LANES, LANES))
    for pair in range(PARTS):
        for half in range(2):
            for u in range(PAIR):
                for s in range(SEG_DEV):
                    for v in range(SRC_PART):
                        lane = half * SRC_PART * SEGS + v * SEGS + (pair * PAIR + u) * SEG_DEV + s
                        row = (u * SEG_DEV + s) * HALF_PART + v * (HALF_PART // SRC_PART)
                        pick[pair, half, row, lane] = 1.0
    return pick.astype(ml_dtypes.bfloat16)


def spread_lanes():
    spread = np.zeros((SRC_PART, LANES, 2 * LANES))
    for v in range(SRC_PART):
        for half in range(2):
            for s in range(SEGS):
                lane = half * LANES + s * GROUP
                spread[v, half * SRC_PART * SEGS + v * SEGS + s, lane : lane + GROUP] = 1.0
    return spread.astype(ml_dtypes.bfloat16)


def tile_lanes():
    count = PAIR * SEG_DEV
    order = np.zeros((TPS * LANES, count * LANES // 2))
    for t in range(TPS):
        for s in range(count):
            for c in range(HALF_PART):
                lane = s * (LANES // 2) + t * HALF_PART + c
                order[t * LANES + s * HALF_PART + c, lane] = 1.0
    return order.astype(ml_dtypes.bfloat16)


PACK_BLOCKS = 8
PACK_STEPS = NB // PACK_BLOCKS


def bits(value, shift, count):
    return jnp.bitwise_and(jnp.right_shift(value, shift), count - 1)


def pack_kernel(own, time, records, marks, out, order, rows):
    lanes = PACK_BLOCKS * BLOCK
    row = lax.broadcasted_iota(jnp.int32, order.shape, 0)
    lane = lax.broadcasted_iota(jnp.int32, order.shape, 1)
    s, j, part = bits(row, 7, SEG_DEV), bits(row, 5, TM), bits(row, 2, 2)
    at = bits(row, 3, SRC_PART) * SRC_PART + bits(row, 0, SRC_PART)
    part = jnp.bitwise_xor(part, bits(time[0], 0, 2))
    target = j * BLOCK + (part * SEG_DEV + s) * HALF_PART + at
    order[...] = jnp.where(lane == target, 1.0, 0.0).astype(BF16)
    row = lax.broadcasted_iota(jnp.int32, rows.shape, 0)
    lane = lax.broadcasted_iota(jnp.int32, rows.shape, 1)
    s, n = bits(row, 6, SEG_DEV), bits(row, 0, ROWS)
    keep = (lane == n * SEG_DEV + s) & (n < SLAB)
    rows[...] = jnp.where(keep, 1.0, 0.0).astype(BF16)
    mark = jnp.concatenate([marks[s : s + 1, :] for s in range(SEG_DEV)], axis=1)
    mark = jnp.broadcast_to(mark.astype(F32), (16, SEG_DEV * BLOCK)).astype(BF16)
    mark = jnp.dot(mark, order[...], preferred_element_type=F32)[:1]
    row = lax.broadcasted_iota(jnp.int32, (ROWS, SEG_DEV * BLOCK), 0)
    for step in range(PACK_STEPS):
        flat = records[:, :, step * lanes : (step + 1) * lanes].reshape(SLAB * SEG_DEV, lanes)
        flat = jnp.dot(rows[...], flat, preferred_element_type=F32).astype(BF16)
        x = jnp.concatenate(
            [
                jnp.concatenate(
                    [
                        flat[s * ROWS : (s + 1) * ROWS, k * BLOCK : (k + 1) * BLOCK]
                        for s in range(SEG_DEV)
                    ],
                    axis=1,
                )
                for k in range(PACK_BLOCKS)
            ],
            axis=0,
        )
        y = jnp.dot(x, order[...], preferred_element_type=F32)
        for k in range(PACK_BLOCKS):
            index = step * PACK_BLOCKS + k
            extra = jnp.where((row == SLAB) & (own[0] == index), mark, 0.0)
            block = (y[k * ROWS : (k + 1) * ROWS] + extra).astype(BF16)
            for j in range(TM):
                out[index * TM + j] = block[:, j * BLOCK : (j + 1) * BLOCK]


def pack(own, time, records, quality):
    return pl.pallas_call(
        pack_kernel,
        out_shape=jax.ShapeDtypeStruct((NB * TM, ROWS, BLOCK), BF16),
        in_specs=[pl.BlockSpec(memory_space=pltpu.SMEM)] * 2
        + [pl.BlockSpec(memory_space=pltpu.VMEM)] * 2,
        out_specs=pl.BlockSpec(memory_space=pltpu.VMEM),
        scratch_shapes=[
            pltpu.VMEM((SEG_DEV * BLOCK, SEG_DEV * BLOCK), BF16),
            pltpu.VMEM((SEG_DEV * ROWS, SLAB * SEG_DEV), BF16),
        ],
        compiler_params=pltpu.CompilerParams(vmem_limit_bytes=20 * MIB),
        name="pack",
    )(own, time, records.transpose(1, 0, 2), quality)


def whiten_kernel(part, own, slabs, table, inside, inverse_count, *refs):
    lane = lax.broadcasted_iota(jnp.int32, (1, LANES), 1)
    sides = [(lane < LANES // 2).astype(F32), (lane >= LANES // 2).astype(F32)]
    x = []
    for pair in range(PARTS):
        halves = []
        for u in range(PAIR):
            i = pair * PAIR + (u ^ part)
            marks = slabs[pl.ds(own[0], 1), i, pl.ds(48, 16), :][0, SLAB - 48 : SLAB - 47, :]
            keep = (marks.astype(F32) * sides[u]).astype(BF16)
            halves.append(slabs[:, i].reshape(NB * ROWS, BLOCK) * keep)
        x.append(halves[0] + halves[1])
    spectrum = jnp.dot(table[...], jnp.concatenate(x, axis=1), preferred_element_type=F32)
    re = spectrum[:F]
    im = spectrum[F:]
    magnitude = jnp.sqrt(re * re + im * im).astype(BF16)
    level = jnp.dot(inside[...], magnitude, preferred_element_type=F32) * inverse_count[...]
    inverse_level = 1.0 / (level + 1e-6)
    white = refs[-1] if part else refs[1]
    total = jnp.zeros((F, LANES), F32)
    for half, value in ((0, re), (1, im)):
        value = (value * inverse_level).astype(BF16)
        for pair in range(PARTS):
            mine = value[:, pair * LANES : (pair + 1) * LANES]
            white[pair, half] = mine
            if not part:
                total += jnp.dot(mine, refs[0][pair, half], preferred_element_type=F32)
    if not part:
        refs[2][...] = total.astype(BF16)


def whiten(part, own, slabs, constants):
    shapes = [jax.ShapeDtypeStruct((PARTS, 2, F, LANES), BF16)]
    picks = []
    if not part:
        shapes.append(jax.ShapeDtypeStruct((F, LANES), BF16))
        picks.append(source_lanes())
    return pl.pallas_call(
        functools.partial(whiten_kernel, part),
        out_shape=shapes,
        in_specs=[pl.BlockSpec(memory_space=pltpu.SMEM)]
        + [pl.BlockSpec(memory_space=pltpu.VMEM)] * (4 + len(picks)),
        out_specs=[pl.BlockSpec(memory_space=pltpu.VMEM)] * len(shapes),
        compiler_params=pltpu.CompilerParams(vmem_limit_bytes=20 * MIB),
        cost_estimate=pl.CostEstimate(flops=1, bytes_accessed=1, transcendentals=0),
        name="whiten",
    )(own, slabs, *constants, *picks)


def choose_kernel(chan, below, above, *refs):
    outs, sem = refs[:-1], refs[-1]
    odd = lax.rem(chan[0], 2)
    count = below.shape[0] // len(outs)
    for index, out in enumerate(outs):
        for parity, ref in ((1, below), (0, above)):

            @pl.when(odd == parity)
            def _():
                part = ref.at[pl.ds(index * count, count)]
                pltpu.make_async_copy(part, out, sem.at[index]).start()

    for index, out in enumerate(outs):
        part = below.at[pl.ds(index * count, count)]
        pltpu.make_async_copy(part, out, sem.at[index]).wait()


def choose(chan, below, above, parts):
    shape = (below.shape[0] // parts, *below.shape[1:])
    return pl.pallas_call(
        choose_kernel,
        out_shape=[jax.ShapeDtypeStruct(shape, below.dtype)] * parts,
        in_specs=[pl.BlockSpec(memory_space=pltpu.SMEM)]
        + [pl.BlockSpec(memory_space=pl.ANY)] * 2,
        out_specs=[pl.BlockSpec(memory_space=pl.ANY)] * parts,
        scratch_shapes=[pltpu.SemaphoreType.DMA((parts,))],
        compiler_params=pltpu.CompilerParams(vmem_limit_bytes=MIB),
        cost_estimate=pl.CostEstimate(flops=1, bytes_accessed=1, transcendentals=0),
        name="choose",
    )(chan, below, above)


def diagonal_kernel(s0, s1, s2, s3, spread, out):
    row = lax.broadcasted_iota(jnp.int32, (F, 2 * LANES), 0)
    lane = lax.broadcasted_iota(jnp.int32, (F, 2 * LANES), 1)
    keep = jnp.bitwise_and(row, GROUP - 1) == jnp.bitwise_and(lane, GROUP - 1)
    for rel, ref in enumerate((s0, s1, s2, s3)):
        for pair in range(SRC_PART // 2):
            wides = []
            for v in (2 * pair, 2 * pair + 1):
                wide = jnp.dot(ref[...], spread[v], preferred_element_type=F32)
                wide = jnp.where(keep, wide, 0.0)
                wides.append(wide.reshape(F // GROUP, GROUP, 2 * LANES))
            at = (rel * SRC_PART + 2 * pair) * GROUP
            out[:, at : at + 2 * GROUP, :] = jnp.concatenate(wides, axis=1).astype(BF16)


def diagonal(sources):
    return pl.pallas_call(
        diagonal_kernel,
        out_shape=jax.ShapeDtypeStruct((F // GROUP, SOURCES * GROUP, 2 * LANES), BF16),
        in_specs=[pl.BlockSpec(memory_space=pltpu.VMEM)] * (TM + 1),
        out_specs=pl.BlockSpec(memory_space=pltpu.VMEM),
        compiler_params=pltpu.CompilerParams(vmem_limit_bytes=20 * MIB),
        cost_estimate=pl.CostEstimate(flops=1, bytes_accessed=1, transcendentals=0),
        name="diagonal",
    )(*sources, spread_lanes())


RECEIVERS = 2 * REACH + 1


def chosen(chan, tiles, t):
    offset = lax.rem(tiles[1, chan * TPS + t] - chan + REACH + NB, NB)
    mate = jnp.where(lax.rem(chan, 2) == 1, 1, 3)
    near = jnp.where(offset == REACH, 0, jnp.where(offset == mate, 3, 4))
    return jnp.where(offset == 0, 1, jnp.where(offset == 2 * REACH, 2, near))


def cross_kernel(part, chan, tiles, diag, order, *refs):
    receivers, (out, held, wide, sem) = refs[:-4], refs[-4:]
    step = pl.program_id(0)
    steps = F // STEP

    def copy(index, t, k):
        rows = pl.ds(k * STEP, STEP)
        refs = receivers[index:] if index == RECEIVERS - 1 else receivers[index : index + 1]
        count = held.shape[2] // len(refs)
        return [
            pltpu.make_async_copy(
                ref.at[:, :, rows, :], held.at[k, t, pl.ds(part * count, count)], sem.at[k, t]
            )
            for part, ref in enumerate(refs)
        ]

    @pl.when(step == 0)
    def _():
        picks = [chosen(chan[0], tiles, t) for t in range(TPS)]
        for k in range(steps):
            for t in range(TPS):
                for index in range(RECEIVERS):

                    @pl.when(picks[t] == index)
                    def _():
                        for one in copy(index, t, k):
                            one.start()

    for t in range(TPS):
        copy(0, t, step)[0].wait()
    x = jnp.concatenate(
        [held[step, t].reshape(TM // PAIR * 2 * STEP, LANES) for t in range(TPS)], axis=1
    )
    y = jnp.dot(x, order[...], preferred_element_type=F32)
    count = PAIR * SEG_DEV
    left = lax.broadcasted_iota(jnp.int32, (STEP, LANES), 1) < LANES // 2
    for i in range(TM // PAIR):
        at = i * 2 * STEP
        for s in range(0, count, 2):
            lanes = slice(s * LANES // 2, s * LANES // 2 + LANES)
            re = y[at : at + STEP, lanes]
            im = y[at + STEP : at + 2 * STEP, lanes]
            re_turned = pltpu.roll(re, LANES // 2, 1)
            im_turned = pltpu.roll(im, LANES // 2, 1)
            index = i * count + (s ^ (part * SEG_DEV))
            wide[index] = jnp.where(left, re, im_turned)
            wide[index + 1] = jnp.where(left, re_turned, im)
            wide[SEGS + index] = jnp.where(left, im, -re_turned)
            wide[SEGS + index + 1] = jnp.where(left, im_turned, -re)
    first = lax.broadcasted_iota(jnp.int32, (1, GROUP, LANES), 2) < LANES // 2

    def group(pair, carry):
        parts = [], []
        for g in range(2):
            at = pl.multiple_of((pair * 2 + g) * GROUP, GROUP)
            b = wide[:, pl.ds(at, GROUP), :].reshape(2 * SEGS * GROUP, LANES).astype(BF16)
            o = jnp.dot(
                diag[step * (STEP // GROUP) + pair * 2 + g], b, preferred_element_type=F32
            )
            turned = pltpu.roll(o, LANES // 2, 1).reshape(SOURCES // 2, 2, GROUP, LANES)
            o = o.reshape(SOURCES // 2, 2, GROUP, LANES)
            parts[0].append(jnp.where(first, o[:, 0], turned[:, 1]))
            parts[1].append(jnp.where(first, turned[:, 0], o[:, 1]))
        rows = pl.ds(pl.multiple_of(step * STEP + pair * 2 * GROUP, 2 * GROUP), 2 * GROUP)
        for half in range(2):
            out[:, half, rows, :] = jnp.concatenate(parts[half], axis=1).astype(BF16)
        return carry

    lax.fori_loop(0, STEP // (2 * GROUP), group, 0, unroll=UNROLL)


UNROLL = 8


def cross(part, chan, tiles, diag, receivers):
    return pl.pallas_call(
        functools.partial(cross_kernel, part),
        out_shape=jax.ShapeDtypeStruct((SOURCES // 2, 2, F, LANES), BF16),
        grid_spec=pltpu.PrefetchScalarGridSpec(
            num_scalar_prefetch=2,
            grid=(F // STEP,),
            in_specs=[pl.BlockSpec(memory_space=pltpu.VMEM)] * 2
            + [pl.BlockSpec(memory_space=pl.ANY)] * len(receivers),
            out_specs=pl.BlockSpec(memory_space=pltpu.VMEM),
            scratch_shapes=[
                pltpu.VMEM((F // STEP, TPS, TM // PAIR, 2, STEP, LANES), BF16),
                pltpu.VMEM((2 * SEGS, STEP, LANES), F32),
                pltpu.SemaphoreType.DMA((F // STEP, TPS)),
            ],
        ),
        compiler_params=pltpu.CompilerParams(vmem_limit_bytes=20 * MIB),
        cost_estimate=pl.CostEstimate(flops=1, bytes_accessed=1, transcendentals=0),
        name="cross",
    )(chan, tiles, diag, tile_lanes(), *receivers)


def stack_kernel(rels, spectra, inverse, *outs):
    for rel, out in zip(rels, outs):
        first = rel * SRC_PART // 2
        x = jnp.concatenate(
            [spectra[first + pair].reshape(2 * F, LANES) for pair in range(SRC_PART // 2)], axis=1
        )
        y = jnp.dot(inverse[...], x, preferred_element_type=F32)
        for pair in range(SRC_PART // 2):
            value = y[:, pair * LANES : (pair + 1) * LANES].T.astype(BF16)
            for v in range(2):
                for t in range(TPS):
                    at = (t * SRC_PART + 2 * pair + v) * HALF_PART
                    row = v * (LANES // 2) + t * HALF_PART
                    out[at : at + HALF_PART, :] = value[row : row + HALF_PART, :]


def stack(spectra, rels, inverse):
    rows = TPS * SRC_PART * HALF_PART
    return pl.pallas_call(
        functools.partial(stack_kernel, rels),
        out_shape=[jax.ShapeDtypeStruct((rows, LAG_COUNT), BF16)] * len(rels),
        in_specs=[pl.BlockSpec(memory_space=pltpu.VMEM)] * 2,
        out_specs=[pl.BlockSpec(memory_space=pltpu.VMEM)] * len(rels),
        compiler_params=pltpu.CompilerParams(vmem_limit_bytes=12 * MIB),
        cost_estimate=pl.CostEstimate(flops=1, bytes_accessed=1, transcendentals=0),
        name="stack",
    )(spectra, inverse)


def merge_kernel(*refs):
    pieces, out, sem = refs[:TM], refs[TM], refs[TM + 1]
    rows = pieces[0].shape[0]
    copies = [
        pltpu.make_async_copy(ref, out.at[pl.ds(rel * rows, rows), :], sem.at[rel])
        for rel, ref in enumerate(pieces)
    ]
    for copy in copies:
        copy.start()
    for copy in copies:
        copy.wait()


def merge(pieces):
    rows, width = pieces[0].shape
    return pl.pallas_call(
        merge_kernel,
        out_shape=jax.ShapeDtypeStruct((TM * rows, width), pieces[0].dtype),
        in_specs=[pl.BlockSpec(memory_space=pl.ANY)] * TM,
        out_specs=pl.BlockSpec(memory_space=pl.ANY),
        scratch_shapes=[pltpu.SemaphoreType.DMA((TM,))],
        compiler_params=pltpu.CompilerParams(vmem_limit_bytes=MIB),
        cost_estimate=pl.CostEstimate(flops=1, bytes_accessed=1, transcendentals=0),
        name="merge",
    )(*pieces)


def arrange(time, pieces, t):
    rows = SRC_PART * HALF_PART
    low, pieces = pieces[0], pieces[1:]
    for rel in range(TM):
        halves = []
        for ref, first in ((low, rel * TPS * rows), (pieces[rel], 0)):
            value = ref[first + t * rows : first + (t + 1) * rows, :].astype(F32)
            halves.append(value.reshape(SRC_PART * HALF_PART // 4, 4, LAG_COUNT))
        value = jnp.concatenate(halves, axis=1).reshape(SRC_PART, PART, LAG_COUNT)
        yield pl.multiple_of(lax.rem(time + TM - rel, TM) * PART, PART), value


def home_kernel(owners, chan, time, *refs):
    pieces, out = refs[:-1], refs[-1]
    slot = pl.program_id(0)
    out[...] = jnp.zeros_like(out)
    for t in range(TPS):

        @pl.when(owners[chan[0] * TPS + t] == chan[0] * TCAP + slot)
        def _():
            for at, value in arrange(time[0], pieces, t):
                out[0, :, pl.ds(at, PART), :] = value


def home(owners, chan, time, pieces):
    return pl.pallas_call(
        home_kernel,
        out_shape=jax.ShapeDtypeStruct((TCAP, SRC_PART, BLOCK, LAG_COUNT), F32),
        grid_spec=pltpu.PrefetchScalarGridSpec(
            num_scalar_prefetch=3,
            grid=(TCAP,),
            in_specs=[pl.BlockSpec(memory_space=pltpu.VMEM) for _ in pieces],
            out_specs=pl.BlockSpec((1, SRC_PART, BLOCK, LAG_COUNT), lambda s, *_: (s, 0, 0, 0)),
        ),
        compiler_params=pltpu.CompilerParams(vmem_limit_bytes=10 * MIB),
        cost_estimate=pl.CostEstimate(flops=1, bytes_accessed=1, transcendentals=0),
        name="home",
    )(owners, chan, time, *pieces)


def moved_kernel(owners, chan, time, *refs):
    pieces, (_, out, held, sem) = refs[:-4], refs[-4:]
    source = lax.rem(chan[0] + NB - 1, NB)
    copies = []
    for t in range(TPS):
        slot = owners[source * TPS + t] - chan[0] * TCAP
        mine = (slot >= 0) & (slot < TCAP)
        copy = pltpu.make_async_copy(held.at[t], out.at[jnp.clip(slot, 0, TCAP - 1)], sem.at[t])
        copies.append((mine, copy))

        @pl.when(mine)
        def _():
            for at, value in arrange(time[0], pieces, t):
                held[t, :, pl.ds(at, PART), :] = value
            copy.start()

    for mine, copy in copies:

        @pl.when(mine)
        def _():
            copy.wait()


def moved(owners, chan, time, pieces, result):
    return pl.pallas_call(
        moved_kernel,
        out_shape=jax.ShapeDtypeStruct(result.shape, result.dtype),
        in_specs=[pl.BlockSpec(memory_space=pltpu.SMEM)] * 3
        + [pl.BlockSpec(memory_space=pltpu.VMEM) for _ in pieces]
        + [pl.BlockSpec(memory_space=pl.ANY)],
        out_specs=pl.BlockSpec(memory_space=pl.ANY),
        scratch_shapes=[
            pltpu.VMEM((TPS, SRC_PART, BLOCK, LAG_COUNT), F32),
            pltpu.SemaphoreType.DMA((TPS,)),
        ],
        input_output_aliases={3 + len(pieces): 0},
        compiler_params=pltpu.CompilerParams(vmem_limit_bytes=12 * MIB),
        cost_estimate=pl.CostEstimate(flops=1, bytes_accessed=1, transcendentals=0),
        name="moved",
    )(owners, chan, time, *pieces, result)


def shifted(value, axis, distance):
    count = lax.axis_size(axis)
    return lax.ppermute(value, axis, [(i, (i + distance) % count) for i in range(count)])


def per_device(records, quality, tile_list, tile_slot_owner):
    chan = lax.axis_index("chan").astype(jnp.int32).reshape(1)
    time = lax.axis_index("tm").astype(jnp.int32).reshape(1)
    tiles = tile_list.T
    swap = [(i, i ^ 1) for i in range(NB)]

    slabs = pack(chan, time, records, quality)
    slabs = lax.all_to_all(slabs, ("chan", "tm"), split_axis=0, concat_axis=0, tiled=True)
    slabs = slabs.reshape(NB, TM, ROWS, BLOCK)
    constants = (forward_table(), *smoothing())
    low, sources = whiten(0, chan, slabs, constants)
    sources = [sources] + [shifted(sources, "tm", -rel) for rel in range(1, TM)]

    def halo(white):
        mate = lax.ppermute(white, "chan", swap)
        return [white, shifted(white, "chan", 2), shifted(white, "chan", -2), mate]

    def complete(blocks, parts):
        others = choose(chan, blocks[1], blocks[2], parts)
        return blocks + [lax.ppermute(other, "chan", swap) for other in others]

    inverse = inverse_table()
    order = (2, 0, 1, 3)
    low = halo(low)
    slabs, low[3] = lax.optimization_barrier((slabs, low[3]))
    (high,) = whiten(1, chan, slabs, constants)
    high, sources = lax.optimization_barrier((high, sources))
    high = halo(high)
    diag = diagonal(sources)
    spectra = cross(0, chan, tiles, diag, complete(low, 2))
    parts = stack(spectra, tuple(range(TM)), inverse)
    stay_low = [shifted(part, "tm", rel) if rel else part for rel, part in enumerate(parts)]
    high, _ = lax.optimization_barrier((high, parts))
    high = complete(high, 1)
    spectra = cross(1, chan, tiles, diag, high)
    spectra, stay_low = lax.optimization_barrier((spectra, stay_low))
    merged = merge(stay_low)
    move_low = shifted(merged, "chan", 1)
    stay_high, move_high = [None] * TM, [None] * TM
    for rel in order:
        (part,) = stack(spectra, (rel,), inverse)
        stay_high[rel] = shifted(part, "tm", rel) if rel else part
        if rel == 2:
            stay_high[rel], move_low = lax.optimization_barrier((stay_high[rel], move_low))
        move_high[rel] = shifted(stay_high[rel], "chan", 1)
    result = home(tile_slot_owner, chan, time, [merged] + stay_high)
    return moved(tile_slot_owner, chan, time, [move_low] + move_high, result)


def solution(mesh):
    placed = (P("tm", "chan", None), P("tm", "chan"), P(), P())
    return jax.shard_map(
        per_device,
        mesh=mesh,
        in_specs=placed,
        out_specs=P("chan", "tm", None, None),
        check_vma=False,
    )
```

```python
import functools
import math

import jax
import jax.numpy as jnp
import ml_dtypes
import numpy as np
from jax import lax
from jax.experimental import pallas as pl
from jax.experimental.pallas import tpu as pltpu
from jax.sharding import PartitionSpec as P

L = 1920
F = 768
K0 = 8
HALF = 32
LAG_COUNT = 512
BLOCK = 128
SOURCES = 16
TPS = 3
REACH = 2
SEG_DEV = 4
SEGS = 16
NB = 32
TCAP = 6
TM = 4
SLAB = L // NB
ROWS = 64
PART = BLOCK // TM
SRC_PART = SOURCES // TM
MIB = 1 << 20
LANES = 128
GROUP = 8
STEP = 128
HALF_PART = PART // 2

BF16 = jnp.bfloat16
F32 = jnp.float32


def forward_table():
    n = np.arange(L)[None, :]
    q = K0 + np.arange(F)[:, None]
    angles = (n * q % L) * (2.0 * np.pi / L)
    window = 0.5 - 0.5 * np.cos(np.arange(L) * (2.0 * np.pi / L))
    table = np.concatenate([np.cos(angles), -np.sin(angles)], axis=0) * window[None, :]
    padded = np.zeros((2 * F, NB, ROWS))
    padded[:, :, :SLAB] = table.reshape(2 * F, NB, SLAB)
    return padded.reshape(2 * F, NB * ROWS).astype(ml_dtypes.bfloat16)


def smoothing():
    k = np.arange(F)
    inside = (np.abs(k[:, None] - k[None, :]) <= HALF).astype(np.float64)
    inverse_count = 1.0 / inside.sum(axis=1, keepdims=True)
    return inside.astype(ml_dtypes.bfloat16), inverse_count.astype(np.float32)


def inverse_table():
    q = K0 + np.arange(F)[None, :]
    lag = np.arange(LAG_COUNT)[:, None] - LAG_COUNT // 2
    angles = (q * lag % L) * (2.0 * np.pi / L)
    table = np.concatenate([np.cos(angles), -np.sin(angles)], axis=1) / math.sqrt(SEGS * F)
    return table.astype(ml_dtypes.bfloat16)


PAIR = 2
PARTS = TM // PAIR


def source_lanes():
    pick = np.zeros((PARTS, 2, LANES, LANES))
    for pair in range(PARTS):
        for half in range(2):
            for u in range(PAIR):
                for s in range(SEG_DEV):
                    for v in range(SRC_PART):
                        lane = half * SRC_PART * SEGS + v * SEGS + (pair * PAIR + u) * SEG_DEV + s
                        row = (u * SEG_DEV + s) * HALF_PART + v * (HALF_PART // SRC_PART)
                        pick[pair, half, row, lane] = 1.0
    return pick.astype(ml_dtypes.bfloat16)


def spread_lanes():
    spread = np.zeros((SRC_PART, LANES, 2 * LANES))
    for v in range(SRC_PART):
        for half in range(2):
            for s in range(SEGS):
                lane = half * LANES + s * GROUP
                spread[v, half * SRC_PART * SEGS + v * SEGS + s, lane : lane + GROUP] = 1.0
    return spread.astype(ml_dtypes.bfloat16)


def tile_lanes():
    count = PAIR * SEG_DEV
    order = np.zeros((TPS * LANES, count * LANES // 2))
    for t in range(TPS):
        for s in range(count):
            for c in range(HALF_PART):
                lane = s * (LANES // 2) + t * HALF_PART + c
                order[t * LANES + s * HALF_PART + c, lane] = 1.0
    return order.astype(ml_dtypes.bfloat16)


PACK_BLOCKS = 8
PACK_STEPS = NB // PACK_BLOCKS


def bits(value, shift, count):
    return jnp.bitwise_and(jnp.right_shift(value, shift), count - 1)


def pack_kernel(own, time, records, marks, out, order, rows):
    lanes = PACK_BLOCKS * BLOCK
    row = lax.broadcasted_iota(jnp.int32, order.shape, 0)
    lane = lax.broadcasted_iota(jnp.int32, order.shape, 1)
    s, j, part = bits(row, 7, SEG_DEV), bits(row, 5, TM), bits(row, 2, 2)
    at = bits(row, 3, SRC_PART) * SRC_PART + bits(row, 0, SRC_PART)
    part = jnp.bitwise_xor(part, bits(time[0], 0, 2))
    target = j * BLOCK + (part * SEG_DEV + s) * HALF_PART + at
    order[...] = jnp.where(lane == target, 1.0, 0.0).astype(BF16)
    row = lax.broadcasted_iota(jnp.int32, rows.shape, 0)
    lane = lax.broadcasted_iota(jnp.int32, rows.shape, 1)
    s, n = bits(row, 6, SEG_DEV), bits(row, 0, ROWS)
    keep = (lane == n * SEG_DEV + s) & (n < SLAB)
    rows[...] = jnp.where(keep, 1.0, 0.0).astype(BF16)
    mark = jnp.concatenate([marks[s : s + 1, :] for s in range(SEG_DEV)], axis=1)
    mark = jnp.broadcast_to(mark.astype(F32), (16, SEG_DEV * BLOCK)).astype(BF16)
    mark = jnp.dot(mark, order[...], preferred_element_type=F32)[:1]
    row = lax.broadcasted_iota(jnp.int32, (ROWS, SEG_DEV * BLOCK), 0)
    for step in range(PACK_STEPS):
        flat = records[:, :, step * lanes : (step + 1) * lanes].reshape(SLAB * SEG_DEV, lanes)
        flat = jnp.dot(rows[...], flat, preferred_element_type=F32).astype(BF16)
        x = jnp.concatenate(
            [
                jnp.concatenate(
                    [
                        flat[s * ROWS : (s + 1) * ROWS, k * BLOCK : (k + 1) * BLOCK]
                        for s in range(SEG_DEV)
                    ],
                    axis=1,
                )
                for k in range(PACK_BLOCKS)
            ],
            axis=0,
        )
        y = jnp.dot(x, order[...], preferred_element_type=F32)
        for k in range(PACK_BLOCKS):
            index = step * PACK_BLOCKS + k
            extra = jnp.where((row == SLAB) & (own[0] == index), mark, 0.0)
            block = (y[k * ROWS : (k + 1) * ROWS] + extra).astype(BF16)
            for j in range(TM):
                out[index * TM + j] = block[:, j * BLOCK : (j + 1) * BLOCK]


def pack(own, time, records, quality):
    return pl.pallas_call(
        pack_kernel,
        out_shape=jax.ShapeDtypeStruct((NB * TM, ROWS, BLOCK), BF16),
        in_specs=[pl.BlockSpec(memory_space=pltpu.SMEM)] * 2
        + [pl.BlockSpec(memory_space=pltpu.VMEM)] * 2,
        out_specs=pl.BlockSpec(memory_space=pltpu.VMEM),
        scratch_shapes=[
            pltpu.VMEM((SEG_DEV * BLOCK, SEG_DEV * BLOCK), BF16),
            pltpu.VMEM((SEG_DEV * ROWS, SLAB * SEG_DEV), BF16),
        ],
        compiler_params=pltpu.CompilerParams(vmem_limit_bytes=20 * MIB),
        name="pack",
    )(own, time, records.transpose(1, 0, 2), quality)


def whiten_kernel(part, own, slabs, table, inside, inverse_count, *refs):
    lane = lax.broadcasted_iota(jnp.int32, (1, LANES), 1)
    sides = [(lane < LANES // 2).astype(F32), (lane >= LANES // 2).astype(F32)]
    x = []
    for pair in range(PARTS):
        halves = []
        for u in range(PAIR):
            i = pair * PAIR + (u ^ part)
            marks = slabs[pl.ds(own[0], 1), i, pl.ds(48, 16), :][0, SLAB - 48 : SLAB - 47, :]
            keep = (marks.astype(F32) * sides[u]).astype(BF16)
            halves.append(slabs[:, i].reshape(NB * ROWS, BLOCK) * keep)
        x.append(halves[0] + halves[1])
    spectrum = jnp.dot(table[...], jnp.concatenate(x, axis=1), preferred_element_type=F32)
    re = spectrum[:F]
    im = spectrum[F:]
    magnitude = jnp.sqrt(re * re + im * im).astype(BF16)
    level = jnp.dot(inside[...], magnitude, preferred_element_type=F32) * inverse_count[...]
    inverse_level = 1.0 / (level + 1e-6)
    white = refs[-1] if part else refs[1]
    total = jnp.zeros((F, LANES), F32)
    for half, value in ((0, re), (1, im)):
        value = (value * inverse_level).astype(BF16)
        for pair in range(PARTS):
            mine = value[:, pair * LANES : (pair + 1) * LANES]
            white[pair, half] = mine
            if not part:
                total += jnp.dot(mine, refs[0][pair, half], preferred_element_type=F32)
    if not part:
        refs[2][...] = total.astype(BF16)


def whiten(part, own, slabs, constants):
    shapes = [jax.ShapeDtypeStruct((PARTS, 2, F, LANES), BF16)]
    picks = []
    if not part:
        shapes.append(jax.ShapeDtypeStruct((F, LANES), BF16))
        picks.append(source_lanes())
    return pl.pallas_call(
        functools.partial(whiten_kernel, part),
        out_shape=shapes,
        in_specs=[pl.BlockSpec(memory_space=pltpu.SMEM)]
        + [pl.BlockSpec(memory_space=pltpu.VMEM)] * (4 + len(picks)),
        out_specs=[pl.BlockSpec(memory_space=pltpu.VMEM)] * len(shapes),
        compiler_params=pltpu.CompilerParams(vmem_limit_bytes=20 * MIB),
        cost_estimate=pl.CostEstimate(flops=1, bytes_accessed=1, transcendentals=0),
        name="whiten",
    )(own, slabs, *constants, *picks)


def choose_kernel(chan, below, above, *refs):
    outs, sem = refs[:-1], refs[-1]
    odd = lax.rem(chan[0], 2)
    count = below.shape[0] // len(outs)
    for index, out in enumerate(outs):
        for parity, ref in ((1, below), (0, above)):

            @pl.when(odd == parity)
            def _():
                part = ref.at[pl.ds(index * count, count)]
                pltpu.make_async_copy(part, out, sem.at[index]).start()

    for index, out in enumerate(outs):
        part = below.at[pl.ds(index * count, count)]
        pltpu.make_async_copy(part, out, sem.at[index]).wait()


def choose(chan, below, above, parts):
    shape = (below.shape[0] // parts, *below.shape[1:])
    return pl.pallas_call(
        choose_kernel,
        out_shape=[jax.ShapeDtypeStruct(shape, below.dtype)] * parts,
        in_specs=[pl.BlockSpec(memory_space=pltpu.SMEM)]
        + [pl.BlockSpec(memory_space=pl.ANY)] * 2,
        out_specs=[pl.BlockSpec(memory_space=pl.ANY)] * parts,
        scratch_shapes=[pltpu.SemaphoreType.DMA((parts,))],
        compiler_params=pltpu.CompilerParams(vmem_limit_bytes=MIB),
        cost_estimate=pl.CostEstimate(flops=1, bytes_accessed=1, transcendentals=0),
        name="choose",
    )(chan, below, above)


def diagonal_kernel(s0, s1, s2, s3, spread, out):
    row = lax.broadcasted_iota(jnp.int32, (F, 2 * LANES), 0)
    lane = lax.broadcasted_iota(jnp.int32, (F, 2 * LANES), 1)
    keep = jnp.bitwise_and(row, GROUP - 1) == jnp.bitwise_and(lane, GROUP - 1)
    for rel, ref in enumerate((s0, s1, s2, s3)):
        for pair in range(SRC_PART // 2):
            wides = []
            for v in (2 * pair, 2 * pair + 1):
                wide = jnp.dot(ref[...], spread[v], preferred_element_type=F32)
                wide = jnp.where(keep, wide, 0.0)
                wides.append(wide.reshape(F // GROUP, GROUP, 2 * LANES))
            at = (rel * SRC_PART + 2 * pair) * GROUP
            out[:, at : at + 2 * GROUP, :] = jnp.concatenate(wides, axis=1).astype(BF16)


def diagonal(sources):
    return pl.pallas_call(
        diagonal_kernel,
        out_shape=jax.ShapeDtypeStruct((F // GROUP, SOURCES * GROUP, 2 * LANES), BF16),
        in_specs=[pl.BlockSpec(memory_space=pltpu.VMEM)] * (TM + 1),
        out_specs=pl.BlockSpec(memory_space=pltpu.VMEM),
        compiler_params=pltpu.CompilerParams(vmem_limit_bytes=20 * MIB),
        cost_estimate=pl.CostEstimate(flops=1, bytes_accessed=1, transcendentals=0),
        name="diagonal",
    )(*sources, spread_lanes())


RECEIVERS = 2 * REACH + 1


def chosen(chan, tiles, t):
    offset = lax.rem(tiles[1, chan * TPS + t] - chan + REACH + NB, NB)
    mate = jnp.where(lax.rem(chan, 2) == 1, 1, 3)
    near = jnp.where(offset == REACH, 0, jnp.where(offset == mate, 3, 4))
    return jnp.where(offset == 0, 1, jnp.where(offset == 2 * REACH, 2, near))


def cross_kernel(part, chan, tiles, diag, order, *refs):
    receivers, (out, held, wide, sem) = refs[:-4], refs[-4:]
    step = pl.program_id(0)
    steps = F // STEP

    def copy(index, t, k):
        rows = pl.ds(k * STEP, STEP)
        refs = receivers[index:] if index == RECEIVERS - 1 else receivers[index : index + 1]
        count = held.shape[2] // len(refs)
        return [
            pltpu.make_async_copy(
                ref.at[:, :, rows, :], held.at[k, t, pl.ds(part * count, count)], sem.at[k, t]
            )
            for part, ref in enumerate(refs)
        ]

    @pl.when(step == 0)
    def _():
        picks = [chosen(chan[0], tiles, t) for t in range(TPS)]
        for k in range(steps):
            for t in range(TPS):
                for index in range(RECEIVERS):

                    @pl.when(picks[t] == index)
                    def _():
                        for one in copy(index, t, k):
                            one.start()

    for t in range(TPS):
        copy(0, t, step)[0].wait()
    x = jnp.concatenate(
        [held[step, t].reshape(TM // PAIR * 2 * STEP, LANES) for t in range(TPS)], axis=1
    )
    y = jnp.dot(x, order[...], preferred_element_type=F32)
    count = PAIR * SEG_DEV
    left = lax.broadcasted_iota(jnp.int32, (STEP, LANES), 1) < LANES // 2
    for i in range(TM // PAIR):
        at = i * 2 * STEP
        for s in range(0, count, 2):
            lanes = slice(s * LANES // 2, s * LANES // 2 + LANES)
            re = y[at : at + STEP, lanes]
            im = y[at + STEP : at + 2 * STEP, lanes]
            re_turned = pltpu.roll(re, LANES // 2, 1)
            im_turned = pltpu.roll(im, LANES // 2, 1)
            index = i * count + (s ^ (part * SEG_DEV))
            wide[index] = jnp.where(left, re, im_turned)
            wide[index + 1] = jnp.where(left, re_turned, im)
            wide[SEGS + index] = jnp.where(left, im, -re_turned)
            wide[SEGS + index + 1] = jnp.where(left, im_turned, -re)
    first = lax.broadcasted_iota(jnp.int32, (1, GROUP, LANES), 2) < LANES // 2

    def group(pair, carry):
        parts = [], []
        for g in range(2):
            at = pl.multiple_of((pair * 2 + g) * GROUP, GROUP)
            b = wide[:, pl.ds(at, GROUP), :].reshape(2 * SEGS * GROUP, LANES).astype(BF16)
            o = jnp.dot(
                diag[step * (STEP // GROUP) + pair * 2 + g], b, preferred_element_type=F32
            )
            turned = pltpu.roll(o, LANES // 2, 1).reshape(SOURCES // 2, 2, GROUP, LANES)
            o = o.reshape(SOURCES // 2, 2, GROUP, LANES)
            parts[0].append(jnp.where(first, o[:, 0], turned[:, 1]))
            parts[1].append(jnp.where(first, turned[:, 0], o[:, 1]))
        rows = pl.ds(pl.multiple_of(step * STEP + pair * 2 * GROUP, 2 * GROUP), 2 * GROUP)
        for half in range(2):
            out[:, half, rows, :] = jnp.concatenate(parts[half], axis=1).astype(BF16)
        return carry

    lax.fori_loop(0, STEP // (2 * GROUP), group, 0, unroll=UNROLL)


UNROLL = 8


def cross(part, chan, tiles, diag, receivers):
    return pl.pallas_call(
        functools.partial(cross_kernel, part),
        out_shape=jax.ShapeDtypeStruct((SOURCES // 2, 2, F, LANES), BF16),
        grid_spec=pltpu.PrefetchScalarGridSpec(
            num_scalar_prefetch=2,
            grid=(F // STEP,),
            in_specs=[pl.BlockSpec(memory_space=pltpu.VMEM)] * 2
            + [pl.BlockSpec(memory_space=pl.ANY)] * len(receivers),
            out_specs=pl.BlockSpec(memory_space=pltpu.VMEM),
            scratch_shapes=[
                pltpu.VMEM((F // STEP, TPS, TM // PAIR, 2, STEP, LANES), BF16),
                pltpu.VMEM((2 * SEGS, STEP, LANES), F32),
                pltpu.SemaphoreType.DMA((F // STEP, TPS)),
            ],
        ),
        compiler_params=pltpu.CompilerParams(vmem_limit_bytes=20 * MIB),
        cost_estimate=pl.CostEstimate(flops=1, bytes_accessed=1, transcendentals=0),
        name="cross",
    )(chan, tiles, diag, tile_lanes(), *receivers)


def stack_kernel(rels, spectra, inverse, *outs):
    for rel, out in zip(rels, outs):
        first = rel * SRC_PART // 2
        x = jnp.concatenate(
            [spectra[first + pair].reshape(2 * F, LANES) for pair in range(SRC_PART // 2)], axis=1
        )
        y = jnp.dot(inverse[...], x, preferred_element_type=F32)
        for pair in range(SRC_PART // 2):
            value = y[:, pair * LANES : (pair + 1) * LANES].T.astype(BF16)
            for v in range(2):
                for t in range(TPS):
                    at = (t * SRC_PART + 2 * pair + v) * HALF_PART
                    row = v * (LANES // 2) + t * HALF_PART
                    out[at : at + HALF_PART, :] = value[row : row + HALF_PART, :]


def stack(spectra, rels, inverse):
    rows = TPS * SRC_PART * HALF_PART
    return pl.pallas_call(
        functools.partial(stack_kernel, rels),
        out_shape=[jax.ShapeDtypeStruct((rows, LAG_COUNT), BF16)] * len(rels),
        in_specs=[pl.BlockSpec(memory_space=pltpu.VMEM)] * 2,
        out_specs=[pl.BlockSpec(memory_space=pltpu.VMEM)] * len(rels),
        compiler_params=pltpu.CompilerParams(vmem_limit_bytes=12 * MIB),
        cost_estimate=pl.CostEstimate(flops=1, bytes_accessed=1, transcendentals=0),
        name="stack",
    )(spectra, inverse)


def merge_kernel(*refs):
    pieces, out, sem = refs[:TM], refs[TM], refs[TM + 1]
    rows = pieces[0].shape[0]
    copies = [
        pltpu.make_async_copy(ref, out.at[pl.ds(rel * rows, rows), :], sem.at[rel])
        for rel, ref in enumerate(pieces)
    ]
    for copy in copies:
        copy.start()
    for copy in copies:
        copy.wait()


def merge(pieces):
    rows, width = pieces[0].shape
    return pl.pallas_call(
        merge_kernel,
        out_shape=jax.ShapeDtypeStruct((TM * rows, width), pieces[0].dtype),
        in_specs=[pl.BlockSpec(memory_space=pl.ANY)] * TM,
        out_specs=pl.BlockSpec(memory_space=pl.ANY),
        scratch_shapes=[pltpu.SemaphoreType.DMA((TM,))],
        compiler_params=pltpu.CompilerParams(vmem_limit_bytes=MIB),
        cost_estimate=pl.CostEstimate(flops=1, bytes_accessed=1, transcendentals=0),
        name="merge",
    )(*pieces)


def arrange(time, low, pieces, rels, t):
    rows = SRC_PART * HALF_PART
    for rel, piece in zip(rels, pieces):
        halves = []
        for ref, first in ((low, rel * TPS * rows), (piece, 0)):
            value = ref[first + t * rows : first + (t + 1) * rows, :].astype(F32)
            halves.append(value.reshape(SRC_PART * HALF_PART // 4, 4, LAG_COUNT))
        value = jnp.concatenate(halves, axis=1).reshape(SRC_PART, PART, LAG_COUNT)
        yield pl.multiple_of(lax.rem(time + TM - rel, TM) * PART, PART), value


def home_kernel(owners, chan, time, *refs):
    pieces, out = refs[:-1], refs[-1]
    slot = pl.program_id(0)
    out[...] = jnp.zeros_like(out)
    for t in range(TPS):

        @pl.when(owners[chan[0] * TPS + t] == chan[0] * TCAP + slot)
        def _():
            for at, value in arrange(time[0], pieces[0], pieces[1:], range(TM), t):
                out[0, :, pl.ds(at, PART), :] = value


def home(owners, chan, time, pieces):
    return pl.pallas_call(
        home_kernel,
        out_shape=jax.ShapeDtypeStruct((TCAP, SRC_PART, BLOCK, LAG_COUNT), F32),
        grid_spec=pltpu.PrefetchScalarGridSpec(
            num_scalar_prefetch=3,
            grid=(TCAP,),
            in_specs=[pl.BlockSpec(memory_space=pltpu.VMEM) for _ in pieces],
            out_specs=pl.BlockSpec((1, SRC_PART, BLOCK, LAG_COUNT), lambda s, *_: (s, 0, 0, 0)),
        ),
        compiler_params=pltpu.CompilerParams(vmem_limit_bytes=10 * MIB),
        cost_estimate=pl.CostEstimate(flops=1, bytes_accessed=1, transcendentals=0),
        name="home",
    )(owners, chan, time, *pieces)


def moved_kernel(rels, owners, chan, time, *refs):
    (low, *pieces), (_, out, held, sem) = refs[:-4], refs[-4:]
    source = lax.rem(chan[0] + NB - 1, NB)
    copies = []
    for t in range(TPS):
        slot = owners[source * TPS + t] - chan[0] * TCAP
        mine = (slot >= 0) & (slot < TCAP)
        place = out.at[jnp.clip(slot, 0, TCAP - 1)]

        @pl.when(mine)
        def _():
            for index, (at, value) in enumerate(arrange(time[0], low, pieces, rels, t)):
                held[t, index] = value
                part = place.at[:, pl.ds(at, PART), :]
                pltpu.make_async_copy(held.at[t, index], part, sem.at[t, index]).start()

        copies.append((mine, place, t))

    for mine, place, t in copies:

        @pl.when(mine)
        def _():
            for index in range(len(rels)):
                part = place.at[:, pl.ds(0, PART), :]
                pltpu.make_async_copy(held.at[t, index], part, sem.at[t, index]).wait()


def moved(rels, owners, chan, time, pieces, result):
    return pl.pallas_call(
        functools.partial(moved_kernel, rels),
        out_shape=jax.ShapeDtypeStruct(result.shape, result.dtype),
        in_specs=[pl.BlockSpec(memory_space=pltpu.SMEM)] * 3
        + [pl.BlockSpec(memory_space=pltpu.VMEM) for _ in pieces]
        + [pl.BlockSpec(memory_space=pl.ANY)],
        out_specs=pl.BlockSpec(memory_space=pl.ANY),
        scratch_shapes=[
            pltpu.VMEM((TPS, len(rels), SRC_PART, PART, LAG_COUNT), F32),
            pltpu.SemaphoreType.DMA((TPS, len(rels))),
        ],
        input_output_aliases={3 + len(pieces): 0},
        compiler_params=pltpu.CompilerParams(vmem_limit_bytes=12 * MIB),
        cost_estimate=pl.CostEstimate(flops=1, bytes_accessed=1, transcendentals=0),
        name="moved",
    )(owners, chan, time, *pieces, result)


def shifted(value, axis, distance):
    count = lax.axis_size(axis)
    return lax.ppermute(value, axis, [(i, (i + distance) % count) for i in range(count)])


def per_device(records, quality, tile_list, tile_slot_owner):
    chan = lax.axis_index("chan").astype(jnp.int32).reshape(1)
    time = lax.axis_index("tm").astype(jnp.int32).reshape(1)
    tiles = tile_list.T
    swap = [(i, i ^ 1) for i in range(NB)]

    slabs = pack(chan, time, records, quality)
    slabs = lax.all_to_all(slabs, ("chan", "tm"), split_axis=0, concat_axis=0, tiled=True)
    slabs = slabs.reshape(NB, TM, ROWS, BLOCK)
    constants = (forward_table(), *smoothing())
    low, sources = whiten(0, chan, slabs, constants)
    sources = [sources] + [shifted(sources, "tm", -rel) for rel in range(1, TM)]

    def halo(white):
        mate = lax.ppermute(white, "chan", swap)
        return [white, shifted(white, "chan", 2), shifted(white, "chan", -2), mate]

    def complete(blocks, parts):
        others = choose(chan, blocks[1], blocks[2], parts)
        return blocks + [lax.ppermute(other, "chan", swap) for other in others]

    inverse = inverse_table()
    order = (2, 0, 1, 3)
    low = halo(low)
    slabs, low[3] = lax.optimization_barrier((slabs, low[3]))
    (high,) = whiten(1, chan, slabs, constants)
    high, sources = lax.optimization_barrier((high, sources))
    high = halo(high)
    diag = diagonal(sources)
    spectra = cross(0, chan, tiles, diag, complete(low, 2))
    parts = stack(spectra, tuple(range(TM)), inverse)
    stay_low = [shifted(part, "tm", rel) if rel else part for rel, part in enumerate(parts)]
    high, _ = lax.optimization_barrier((high, parts))
    high = complete(high, 1)
    spectra = cross(1, chan, tiles, diag, high)
    spectra, stay_low = lax.optimization_barrier((spectra, stay_low))
    merged = merge(stay_low)
    move_low = shifted(merged, "chan", 1)
    stay_high, move_high = [None] * TM, [None] * TM
    for rel in order:
        (part,) = stack(spectra, (rel,), inverse)
        stay_high[rel] = shifted(part, "tm", rel) if rel else part
        move_high[rel] = shifted(stay_high[rel], "chan", 1)
    stay_high, move_low = lax.optimization_barrier((stay_high, move_low))
    result = home(tile_slot_owner, chan, time, [merged] + stay_high)
    for rels in ((0, 2, 1), (3,)):
        pieces = [move_low] + [move_high[rel] for rel in rels]
        result = moved(rels, tile_slot_owner, chan, time, pieces, result)
    return result


def solution(mesh):
    placed = (P("tm", "chan", None), P("tm", "chan"), P(), P())
    return jax.shard_map(
        per_device,
        mesh=mesh,
        in_specs=placed,
        out_specs=P("chan", "tm", None, None),
        check_vma=False,
    )
```

```python
import functools
import math

import jax
import jax.numpy as jnp
import ml_dtypes
import numpy as np
from jax import lax
from jax.experimental import pallas as pl
from jax.experimental.pallas import tpu as pltpu
from jax.sharding import PartitionSpec as P

L = 1920
F = 768
K0 = 8
HALF = 32
LAG_COUNT = 512
BLOCK = 128
SOURCES = 16
TPS = 3
REACH = 2
SEG_DEV = 4
SEGS = 16
NB = 32
TCAP = 6
TM = 4
SLAB = L // NB
ROWS = 64
PART = BLOCK // TM
SRC_PART = SOURCES // TM
MIB = 1 << 20
LANES = 128
GROUP = 8
STEP = 128
HALF_PART = PART // 2

BF16 = jnp.bfloat16
F32 = jnp.float32


def forward_table():
    n = np.arange(L)[None, :]
    q = K0 + np.arange(F)[:, None]
    angles = (n * q % L) * (2.0 * np.pi / L)
    window = 0.5 - 0.5 * np.cos(np.arange(L) * (2.0 * np.pi / L))
    table = np.concatenate([np.cos(angles), -np.sin(angles)], axis=0) * window[None, :]
    padded = np.zeros((2 * F, NB, ROWS))
    padded[:, :, :SLAB] = table.reshape(2 * F, NB, SLAB)
    return padded.reshape(2 * F, NB * ROWS).astype(ml_dtypes.bfloat16)


def smoothing():
    k = np.arange(F)
    inside = (np.abs(k[:, None] - k[None, :]) <= HALF).astype(np.float64)
    inverse_count = 1.0 / inside.sum(axis=1, keepdims=True)
    return inside.astype(ml_dtypes.bfloat16), inverse_count.astype(np.float32)


def inverse_table():
    q = K0 + np.arange(F)[None, :]
    lag = np.arange(LAG_COUNT)[:, None] - LAG_COUNT // 2
    angles = (q * lag % L) * (2.0 * np.pi / L)
    table = np.concatenate([np.cos(angles), -np.sin(angles)], axis=1) / math.sqrt(SEGS * F)
    return table.astype(ml_dtypes.bfloat16)


PAIR = 2
PARTS = TM // PAIR


def source_lanes():
    pick = np.zeros((PARTS, 2, LANES, LANES))
    for pair in range(PARTS):
        for half in range(2):
            for u in range(PAIR):
                for s in range(SEG_DEV):
                    for v in range(SRC_PART):
                        lane = half * SRC_PART * SEGS + v * SEGS + (pair * PAIR + u) * SEG_DEV + s
                        row = (u * SEG_DEV + s) * HALF_PART + v * (HALF_PART // SRC_PART)
                        pick[pair, half, row, lane] = 1.0
    return pick.astype(ml_dtypes.bfloat16)


def spread_lanes():
    spread = np.zeros((SRC_PART, LANES, 2 * LANES))
    for v in range(SRC_PART):
        for half in range(2):
            for s in range(SEGS):
                lane = half * LANES + s * GROUP
                spread[v, half * SRC_PART * SEGS + v * SEGS + s, lane : lane + GROUP] = 1.0
    return spread.astype(ml_dtypes.bfloat16)


def tile_lanes():
    count = PAIR * SEG_DEV
    order = np.zeros((TPS * LANES, count * LANES // 2))
    for t in range(TPS):
        for s in range(count):
            for c in range(HALF_PART):
                lane = s * (LANES // 2) + t * HALF_PART + c
                order[t * LANES + s * HALF_PART + c, lane] = 1.0
    return order.astype(ml_dtypes.bfloat16)


PACK_BLOCKS = 8
PACK_STEPS = NB // PACK_BLOCKS


def bits(value, shift, count):
    return jnp.bitwise_and(jnp.right_shift(value, shift), count - 1)


def pack_kernel(own, time, records, marks, out, order, rows):
    lanes = PACK_BLOCKS * BLOCK
    row = lax.broadcasted_iota(jnp.int32, order.shape, 0)
    lane = lax.broadcasted_iota(jnp.int32, order.shape, 1)
    s, j, part = bits(row, 7, SEG_DEV), bits(row, 5, TM), bits(row, 2, 2)
    at = bits(row, 3, SRC_PART) * SRC_PART + bits(row, 0, SRC_PART)
    part = jnp.bitwise_xor(part, bits(time[0], 0, 2))
    target = j * BLOCK + (part * SEG_DEV + s) * HALF_PART + at
    order[...] = jnp.where(lane == target, 1.0, 0.0).astype(BF16)
    row = lax.broadcasted_iota(jnp.int32, rows.shape, 0)
    lane = lax.broadcasted_iota(jnp.int32, rows.shape, 1)
    s, n = bits(row, 6, SEG_DEV), bits(row, 0, ROWS)
    keep = (lane == n * SEG_DEV + s) & (n < SLAB)
    rows[...] = jnp.where(keep, 1.0, 0.0).astype(BF16)
    mark = jnp.concatenate([marks[s : s + 1, :] for s in range(SEG_DEV)], axis=1)
    mark = jnp.broadcast_to(mark.astype(F32), (16, SEG_DEV * BLOCK)).astype(BF16)
    mark = jnp.dot(mark, order[...], preferred_element_type=F32)[:1]
    row = lax.broadcasted_iota(jnp.int32, (ROWS, SEG_DEV * BLOCK), 0)
    for step in range(PACK_STEPS):
        flat = records[:, :, step * lanes : (step + 1) * lanes].reshape(SLAB * SEG_DEV, lanes)
        flat = jnp.dot(rows[...], flat, preferred_element_type=F32).astype(BF16)
        x = jnp.concatenate(
            [
                jnp.concatenate(
                    [
                        flat[s * ROWS : (s + 1) * ROWS, k * BLOCK : (k + 1) * BLOCK]
                        for s in range(SEG_DEV)
                    ],
                    axis=1,
                )
                for k in range(PACK_BLOCKS)
            ],
            axis=0,
        )
        y = jnp.dot(x, order[...], preferred_element_type=F32)
        for k in range(PACK_BLOCKS):
            index = step * PACK_BLOCKS + k
            extra = jnp.where((row == SLAB) & (own[0] == index), mark, 0.0)
            block = (y[k * ROWS : (k + 1) * ROWS] + extra).astype(BF16)
            for j in range(TM):
                out[index * TM + j] = block[:, j * BLOCK : (j + 1) * BLOCK]


def pack(own, time, records, quality):
    return pl.pallas_call(
        pack_kernel,
        out_shape=jax.ShapeDtypeStruct((NB * TM, ROWS, BLOCK), BF16),
        in_specs=[pl.BlockSpec(memory_space=pltpu.SMEM)] * 2
        + [pl.BlockSpec(memory_space=pltpu.VMEM)] * 2,
        out_specs=pl.BlockSpec(memory_space=pltpu.VMEM),
        scratch_shapes=[
            pltpu.VMEM((SEG_DEV * BLOCK, SEG_DEV * BLOCK), BF16),
            pltpu.VMEM((SEG_DEV * ROWS, SLAB * SEG_DEV), BF16),
        ],
        compiler_params=pltpu.CompilerParams(vmem_limit_bytes=20 * MIB),
        name="pack",
    )(own, time, records.transpose(1, 0, 2), quality)


def whiten_kernel(part, own, slabs, table, inside, inverse_count, *refs):
    lane = lax.broadcasted_iota(jnp.int32, (1, LANES), 1)
    sides = [(lane < LANES // 2).astype(F32), (lane >= LANES // 2).astype(F32)]
    x = []
    for pair in range(PARTS):
        halves = []
        for u in range(PAIR):
            i = pair * PAIR + (u ^ part)
            marks = slabs[pl.ds(own[0], 1), i, pl.ds(48, 16), :][0, SLAB - 48 : SLAB - 47, :]
            keep = (marks.astype(F32) * sides[u]).astype(BF16)
            halves.append(slabs[:, i].reshape(NB * ROWS, BLOCK) * keep)
        x.append(halves[0] + halves[1])
    spectrum = jnp.dot(table[...], jnp.concatenate(x, axis=1), preferred_element_type=F32)
    re = spectrum[:F]
    im = spectrum[F:]
    magnitude = jnp.sqrt(re * re + im * im).astype(BF16)
    level = jnp.dot(inside[...], magnitude, preferred_element_type=F32) * inverse_count[...]
    inverse_level = 1.0 / (level + 1e-6)
    white = refs[-1] if part else refs[1]
    total = jnp.zeros((F, LANES), F32)
    for half, value in ((0, re), (1, im)):
        value = (value * inverse_level).astype(BF16)
        for pair in range(PARTS):
            mine = value[:, pair * LANES : (pair + 1) * LANES]
            white[pair, half] = mine
            if not part:
                total += jnp.dot(mine, refs[0][pair, half], preferred_element_type=F32)
    if not part:
        refs[2][...] = total.astype(BF16)


def whiten(part, own, slabs, constants):
    shapes = [jax.ShapeDtypeStruct((PARTS, 2, F, LANES), BF16)]
    picks = []
    if not part:
        shapes.append(jax.ShapeDtypeStruct((F, LANES), BF16))
        picks.append(source_lanes())
    return pl.pallas_call(
        functools.partial(whiten_kernel, part),
        out_shape=shapes,
        in_specs=[pl.BlockSpec(memory_space=pltpu.SMEM)]
        + [pl.BlockSpec(memory_space=pltpu.VMEM)] * (4 + len(picks)),
        out_specs=[pl.BlockSpec(memory_space=pltpu.VMEM)] * len(shapes),
        compiler_params=pltpu.CompilerParams(vmem_limit_bytes=20 * MIB),
        cost_estimate=pl.CostEstimate(flops=1, bytes_accessed=1, transcendentals=0),
        name="whiten",
    )(own, slabs, *constants, *picks)


def choose_kernel(chan, below, above, *refs):
    outs, sem = refs[:-1], refs[-1]
    odd = lax.rem(chan[0], 2)
    count = below.shape[0] // len(outs)
    for index, out in enumerate(outs):
        for parity, ref in ((1, below), (0, above)):

            @pl.when(odd == parity)
            def _():
                part = ref.at[pl.ds(index * count, count)]
                pltpu.make_async_copy(part, out, sem.at[index]).start()

    for index, out in enumerate(outs):
        part = below.at[pl.ds(index * count, count)]
        pltpu.make_async_copy(part, out, sem.at[index]).wait()


def choose(chan, below, above, parts):
    shape = (below.shape[0] // parts, *below.shape[1:])
    return pl.pallas_call(
        choose_kernel,
        out_shape=[jax.ShapeDtypeStruct(shape, below.dtype)] * parts,
        in_specs=[pl.BlockSpec(memory_space=pltpu.SMEM)]
        + [pl.BlockSpec(memory_space=pl.ANY)] * 2,
        out_specs=[pl.BlockSpec(memory_space=pl.ANY)] * parts,
        scratch_shapes=[pltpu.SemaphoreType.DMA((parts,))],
        compiler_params=pltpu.CompilerParams(vmem_limit_bytes=MIB),
        cost_estimate=pl.CostEstimate(flops=1, bytes_accessed=1, transcendentals=0),
        name="choose",
    )(chan, below, above)


def diagonal_kernel(s0, s1, s2, s3, spread, out):
    row = lax.broadcasted_iota(jnp.int32, (F, 2 * LANES), 0)
    lane = lax.broadcasted_iota(jnp.int32, (F, 2 * LANES), 1)
    keep = jnp.bitwise_and(row, GROUP - 1) == jnp.bitwise_and(lane, GROUP - 1)
    for rel, ref in enumerate((s0, s1, s2, s3)):
        for pair in range(SRC_PART // 2):
            wides = []
            for v in (2 * pair, 2 * pair + 1):
                wide = jnp.dot(ref[...], spread[v], preferred_element_type=F32)
                wide = jnp.where(keep, wide, 0.0)
                wides.append(wide.reshape(F // GROUP, GROUP, 2 * LANES))
            at = (rel * SRC_PART + 2 * pair) * GROUP
            out[:, at : at + 2 * GROUP, :] = jnp.concatenate(wides, axis=1).astype(BF16)


def diagonal(sources):
    return pl.pallas_call(
        diagonal_kernel,
        out_shape=jax.ShapeDtypeStruct((F // GROUP, SOURCES * GROUP, 2 * LANES), BF16),
        in_specs=[pl.BlockSpec(memory_space=pltpu.VMEM)] * (TM + 1),
        out_specs=pl.BlockSpec(memory_space=pltpu.VMEM),
        compiler_params=pltpu.CompilerParams(vmem_limit_bytes=20 * MIB),
        cost_estimate=pl.CostEstimate(flops=1, bytes_accessed=1, transcendentals=0),
        name="diagonal",
    )(*sources, spread_lanes())


RECEIVERS = 2 * REACH + 1


def chosen(chan, tiles, t):
    offset = lax.rem(tiles[1, chan * TPS + t] - chan + REACH + NB, NB)
    mate = jnp.where(lax.rem(chan, 2) == 1, 1, 3)
    near = jnp.where(offset == REACH, 0, jnp.where(offset == mate, 3, 4))
    return jnp.where(offset == 0, 1, jnp.where(offset == 2 * REACH, 2, near))


def cross_kernel(part, chan, tiles, diag, order, *refs):
    receivers, (out, held, wide, sem) = refs[:-4], refs[-4:]
    step = pl.program_id(0)
    steps = F // STEP

    def copy(index, t, k):
        rows = pl.ds(k * STEP, STEP)
        refs = receivers[index:] if index == RECEIVERS - 1 else receivers[index : index + 1]
        count = held.shape[2] // len(refs)
        return [
            pltpu.make_async_copy(
                ref.at[:, :, rows, :], held.at[k, t, pl.ds(part * count, count)], sem.at[k, t]
            )
            for part, ref in enumerate(refs)
        ]

    @pl.when(step == 0)
    def _():
        picks = [chosen(chan[0], tiles, t) for t in range(TPS)]
        for k in range(steps):
            for t in range(TPS):
                for index in range(RECEIVERS):

                    @pl.when(picks[t] == index)
                    def _():
                        for one in copy(index, t, k):
                            one.start()

    for t in range(TPS):
        copy(0, t, step)[0].wait()
    x = jnp.concatenate(
        [held[step, t].reshape(TM // PAIR * 2 * STEP, LANES) for t in range(TPS)], axis=1
    )
    y = jnp.dot(x, order[...], preferred_element_type=F32)
    count = PAIR * SEG_DEV
    left = lax.broadcasted_iota(jnp.int32, (STEP, LANES), 1) < LANES // 2
    for i in range(TM // PAIR):
        at = i * 2 * STEP
        for s in range(0, count, 2):
            lanes = slice(s * LANES // 2, s * LANES // 2 + LANES)
            re = y[at : at + STEP, lanes]
            im = y[at + STEP : at + 2 * STEP, lanes]
            re_turned = pltpu.roll(re, LANES // 2, 1)
            im_turned = pltpu.roll(im, LANES // 2, 1)
            index = i * count + (s ^ (part * SEG_DEV))
            wide[index] = jnp.where(left, re, im_turned)
            wide[index + 1] = jnp.where(left, re_turned, im)
            wide[SEGS + index] = jnp.where(left, im, -re_turned)
            wide[SEGS + index + 1] = jnp.where(left, im_turned, -re)
    first = lax.broadcasted_iota(jnp.int32, (1, GROUP, LANES), 2) < LANES // 2

    def group(pair, carry):
        parts = [], []
        for g in range(2):
            at = pl.multiple_of((pair * 2 + g) * GROUP, GROUP)
            b = wide[:, pl.ds(at, GROUP), :].reshape(2 * SEGS * GROUP, LANES).astype(BF16)
            o = jnp.dot(
                diag[step * (STEP // GROUP) + pair * 2 + g], b, preferred_element_type=F32
            )
            turned = pltpu.roll(o, LANES // 2, 1).reshape(SOURCES // 2, 2, GROUP, LANES)
            o = o.reshape(SOURCES // 2, 2, GROUP, LANES)
            parts[0].append(jnp.where(first, o[:, 0], turned[:, 1]))
            parts[1].append(jnp.where(first, turned[:, 0], o[:, 1]))
        rows = pl.ds(pl.multiple_of(step * STEP + pair * 2 * GROUP, 2 * GROUP), 2 * GROUP)
        for half in range(2):
            out[:, half, rows, :] = jnp.concatenate(parts[half], axis=1).astype(BF16)
        return carry

    lax.fori_loop(0, STEP // (2 * GROUP), group, 0, unroll=UNROLL)


UNROLL = 8


def cross(part, chan, tiles, diag, receivers):
    return pl.pallas_call(
        functools.partial(cross_kernel, part),
        out_shape=jax.ShapeDtypeStruct((SOURCES // 2, 2, F, LANES), BF16),
        grid_spec=pltpu.PrefetchScalarGridSpec(
            num_scalar_prefetch=2,
            grid=(F // STEP,),
            in_specs=[pl.BlockSpec(memory_space=pltpu.VMEM)] * 2
            + [pl.BlockSpec(memory_space=pl.ANY)] * len(receivers),
            out_specs=pl.BlockSpec(memory_space=pltpu.VMEM),
            scratch_shapes=[
                pltpu.VMEM((F // STEP, TPS, TM // PAIR, 2, STEP, LANES), BF16),
                pltpu.VMEM((2 * SEGS, STEP, LANES), F32),
                pltpu.SemaphoreType.DMA((F // STEP, TPS)),
            ],
        ),
        compiler_params=pltpu.CompilerParams(vmem_limit_bytes=20 * MIB),
        cost_estimate=pl.CostEstimate(flops=1, bytes_accessed=1, transcendentals=0),
        name="cross",
    )(chan, tiles, diag, tile_lanes(), *receivers)


def stack_kernel(rels, spectra, inverse, *outs):
    for rel, out in zip(rels, outs):
        first = rel * SRC_PART // 2
        x = jnp.concatenate(
            [spectra[first + pair].reshape(2 * F, LANES) for pair in range(SRC_PART // 2)], axis=1
        )
        y = jnp.dot(inverse[...], x, preferred_element_type=F32)
        for pair in range(SRC_PART // 2):
            value = y[:, pair * LANES : (pair + 1) * LANES].T.astype(BF16)
            for v in range(2):
                for t in range(TPS):
                    at = (t * SRC_PART + 2 * pair + v) * HALF_PART
                    row = v * (LANES // 2) + t * HALF_PART
                    out[at : at + HALF_PART, :] = value[row : row + HALF_PART, :]


def stack(spectra, rels, inverse):
    rows = TPS * SRC_PART * HALF_PART
    return pl.pallas_call(
        functools.partial(stack_kernel, rels),
        out_shape=[jax.ShapeDtypeStruct((rows, LAG_COUNT), BF16)] * len(rels),
        in_specs=[pl.BlockSpec(memory_space=pltpu.VMEM)] * 2,
        out_specs=[pl.BlockSpec(memory_space=pltpu.VMEM)] * len(rels),
        compiler_params=pltpu.CompilerParams(vmem_limit_bytes=12 * MIB),
        cost_estimate=pl.CostEstimate(flops=1, bytes_accessed=1, transcendentals=0),
        name="stack",
    )(spectra, inverse)


def merge_kernel(*refs):
    pieces, out, sem = refs[:TM], refs[TM], refs[TM + 1]
    rows = pieces[0].shape[0]
    copies = [
        pltpu.make_async_copy(ref, out.at[pl.ds(rel * rows, rows), :], sem.at[rel])
        for rel, ref in enumerate(pieces)
    ]
    for copy in copies:
        copy.start()
    for copy in copies:
        copy.wait()


def merge(pieces):
    rows, width = pieces[0].shape
    return pl.pallas_call(
        merge_kernel,
        out_shape=jax.ShapeDtypeStruct((TM * rows, width), pieces[0].dtype),
        in_specs=[pl.BlockSpec(memory_space=pl.ANY)] * TM,
        out_specs=pl.BlockSpec(memory_space=pl.ANY),
        scratch_shapes=[pltpu.SemaphoreType.DMA((TM,))],
        compiler_params=pltpu.CompilerParams(vmem_limit_bytes=MIB),
        cost_estimate=pl.CostEstimate(flops=1, bytes_accessed=1, transcendentals=0),
        name="merge",
    )(*pieces)


def arrange(time, low, pieces, rels, t):
    rows = SRC_PART * HALF_PART
    for rel, piece in zip(rels, pieces):
        halves = []
        for ref, first in ((low, rel * TPS * rows), (piece, 0)):
            value = ref[first + t * rows : first + (t + 1) * rows, :].astype(F32)
            halves.append(value.reshape(SRC_PART * HALF_PART // 4, 4, LAG_COUNT))
        value = jnp.concatenate(halves, axis=1).reshape(SRC_PART, PART, LAG_COUNT)
        yield pl.multiple_of(lax.rem(time + TM - rel, TM) * PART, PART), value


def home_kernel(owners, chan, time, *refs):
    pieces, out = refs[:-1], refs[-1]
    slot = pl.program_id(0)
    out[...] = jnp.zeros_like(out)
    for t in range(TPS):

        @pl.when(owners[chan[0] * TPS + t] == chan[0] * TCAP + slot)
        def _():
            for at, value in arrange(time[0], pieces[0], pieces[1:], range(TM), t):
                out[0, :, pl.ds(at, PART), :] = value


def home(owners, chan, time, pieces):
    return pl.pallas_call(
        home_kernel,
        out_shape=jax.ShapeDtypeStruct((TCAP, SRC_PART, BLOCK, LAG_COUNT), F32),
        grid_spec=pltpu.PrefetchScalarGridSpec(
            num_scalar_prefetch=3,
            grid=(TCAP,),
            in_specs=[pl.BlockSpec(memory_space=pltpu.VMEM) for _ in pieces],
            out_specs=pl.BlockSpec((1, SRC_PART, BLOCK, LAG_COUNT), lambda s, *_: (s, 0, 0, 0)),
        ),
        compiler_params=pltpu.CompilerParams(vmem_limit_bytes=10 * MIB),
        cost_estimate=pl.CostEstimate(flops=1, bytes_accessed=1, transcendentals=0),
        name="home",
    )(owners, chan, time, *pieces)


def moved_kernel(rels, owners, chan, time, *refs):
    (low, *pieces), (_, out, held, sem) = refs[:-4], refs[-4:]
    source = lax.rem(chan[0] + NB - 1, NB)
    copies = []
    for t in range(TPS):
        slot = owners[source * TPS + t] - chan[0] * TCAP
        mine = (slot >= 0) & (slot < TCAP)
        place = out.at[jnp.clip(slot, 0, TCAP - 1)]

        @pl.when(mine)
        def _():
            for index, (at, value) in enumerate(arrange(time[0], low, pieces, rels, t)):
                held[t, index] = value
                part = place.at[:, pl.ds(at, PART), :]
                pltpu.make_async_copy(held.at[t, index], part, sem.at[t, index]).start()

        copies.append((mine, place, t))

    for mine, place, t in copies:

        @pl.when(mine)
        def _():
            for index in range(len(rels)):
                part = place.at[:, pl.ds(0, PART), :]
                pltpu.make_async_copy(held.at[t, index], part, sem.at[t, index]).wait()


def moved(rels, owners, chan, time, pieces, result):
    return pl.pallas_call(
        functools.partial(moved_kernel, rels),
        out_shape=jax.ShapeDtypeStruct(result.shape, result.dtype),
        in_specs=[pl.BlockSpec(memory_space=pltpu.SMEM)] * 3
        + [pl.BlockSpec(memory_space=pltpu.VMEM) for _ in pieces]
        + [pl.BlockSpec(memory_space=pl.ANY)],
        out_specs=pl.BlockSpec(memory_space=pl.ANY),
        scratch_shapes=[
            pltpu.VMEM((TPS, len(rels), SRC_PART, PART, LAG_COUNT), F32),
            pltpu.SemaphoreType.DMA((TPS, len(rels))),
        ],
        input_output_aliases={3 + len(pieces): 0},
        compiler_params=pltpu.CompilerParams(vmem_limit_bytes=12 * MIB),
        cost_estimate=pl.CostEstimate(flops=1, bytes_accessed=1, transcendentals=0),
        name="moved",
    )(owners, chan, time, *pieces, result)


def shifted(value, axis, distance):
    count = lax.axis_size(axis)
    return lax.ppermute(value, axis, [(i, (i + distance) % count) for i in range(count)])


def per_device(records, quality, tile_list, tile_slot_owner):
    chan = lax.axis_index("chan").astype(jnp.int32).reshape(1)
    time = lax.axis_index("tm").astype(jnp.int32).reshape(1)
    tiles = tile_list.T
    swap = [(i, i ^ 1) for i in range(NB)]

    slabs = pack(chan, time, records, quality)
    slabs = lax.all_to_all(slabs, ("chan", "tm"), split_axis=0, concat_axis=0, tiled=True)
    slabs = slabs.reshape(NB, TM, ROWS, BLOCK)
    constants = (forward_table(), *smoothing())
    low, sources = whiten(0, chan, slabs, constants)
    sources = [sources] + [shifted(sources, "tm", -rel) for rel in range(1, TM)]

    def halo(white):
        mate = lax.ppermute(white, "chan", swap)
        return [white, shifted(white, "chan", 2), shifted(white, "chan", -2), mate]

    def complete(blocks, parts):
        others = choose(chan, blocks[1], blocks[2], parts)
        return blocks + [lax.ppermute(other, "chan", swap) for other in others]

    inverse = inverse_table()
    order = (2, 0, 1, 3)
    low = halo(low)
    slabs, low[3] = lax.optimization_barrier((slabs, low[3]))
    (high,) = whiten(1, chan, slabs, constants)
    high, sources = lax.optimization_barrier((high, sources))
    high = halo(high)
    diag = diagonal(sources)
    spectra = cross(0, chan, tiles, diag, complete(low, 2))
    parts = stack(spectra, tuple(range(TM)), inverse)
    stay_low = [shifted(part, "tm", rel) if rel else part for rel, part in enumerate(parts)]
    high, _ = lax.optimization_barrier((high, parts))
    high = complete(high, 1)
    spectra = cross(1, chan, tiles, diag, high)
    spectra, stay_low = lax.optimization_barrier((spectra, stay_low))
    merged = merge(stay_low)
    move_low = shifted(merged, "chan", 1)
    stay_high, move_high = [None] * TM, [None] * TM
    parts = dict(zip((2, 1, 3), stack(spectra, (2, 1, 3), inverse)))
    (parts[0],) = stack(spectra, (0,), inverse)
    for rel in order:
        part = parts[rel]
        stay_high[rel] = shifted(part, "tm", rel) if rel else part
        move_high[rel] = shifted(stay_high[rel], "chan", 1)
    stay_high, move_low = lax.optimization_barrier((stay_high, move_low))
    result = home(tile_slot_owner, chan, time, [merged] + stay_high)
    for rels in ((0, 2, 1), (3,)):
        pieces = [move_low] + [move_high[rel] for rel in rels]
        result = moved(rels, tile_slot_owner, chan, time, pieces, result)
    return result


def solution(mesh):
    placed = (P("tm", "chan", None), P("tm", "chan"), P(), P())
    return jax.shard_map(
        per_device,
        mesh=mesh,
        in_specs=placed,
        out_specs=P("chan", "tm", None, None),
        check_vma=False,
    )
```
